128 devices in a mesh: space: 4 (over y_hi, core), chan: 32 (over y_lo, x, z).
Axes of the slice: x: 4, y: 4 (y_hi: 2, y_lo: 2; y = y_hi * 2 + y_lo), z: 4, core: 2. Of those that a mesh axis runs over, the one named last changes fastest.
Arguments:
- point_feats: bfloat16 [262144, 256], P(('space', 'chan')), may hold values from -6 to 6
- send_slots: int32 [4, 32, 4, 1024], P('space', 'chan'), may hold values from 0 to 2047
- send_counts: int32 [4, 32, 4], P('space', 'chan'), may hold values from 1 to 1024, as said below
- neighbors: int32 [16, 32, 32, 128], P('space', 'chan'), may hold values from 0 to 4095, as said below
- tile_fill: int32 [16, 32, 32], P('space', 'chan'), may hold values from 16 to 128
- offsets: float32 [16, 32, 32, 3, 128], P('space', 'chan'), may hold values from -2.5 to 2.5
- weight: bfloat16 [256, 27, 256], P('chan'), may hold values from -0.078125 to 0.078125
- conv_bias: bfloat16 [256], replicated, may hold values from -3 to 3
- cotangent: bfloat16 [16, 128, 128, 256], P('space', 'chan'), may hold values from -6 to 6
Outputs:
- activated: bfloat16 [16, 128, 128, 256], P('space', 'chan')
- weight_grad: float32 [256, 27, 256], P('chan')
The draws below stay inside these ranges and needn't reach their ends.
Inputs may be any that keep to these rules, and one draw needn't show every extreme that they name: `send_counts`: at most 1024 per device and owner; for every index of chan, one owner receives exactly 1024 from every source. `neighbors`: entry (z, a, b, s) is src * 1024 + j for a source index src of space and a slot j < send_counts[src, c, z // 4], with c the tile's index of chan.
All inputs are finite; a program needn't handle non-finite values.
Results may differ from the reference program's by a relative error of at most 0.0059.
Values may be sent and summed in bfloat16 or wider, within the bound.
No kernel may reach another device: no remote copies, remote signals or barrier semaphores. Data moves between devices by JAX's collectives and lax.ppermute only.
A program may use at most 192 MiB of HBM per device.

```python
import math
import jax
import jax.numpy as jnp
from jax import lax

C = 256
CZ = 4
CX = 4
NY = 128
SLOTS = 128
PTS_DEV = 2048
CAP = 1024
NZ = 16
NX = 128
NPTS = 262144
N_SPACE = 4
N_CHAN = 32


def shared_counts(key):
    spaces = NZ // CZ
    chans = NX // CX
    lowest = max(1, CAP // 8)
    counts = jax.random.randint(jax.random.fold_in(key, 11), (spaces, chans, spaces), lowest, CAP // 2 + 1)
    chosen = jax.random.randint(jax.random.fold_in(key, 12), (chans,), 0, spaces)
    column = jnp.arange(spaces)[None, None, :]
    return jnp.where(column == chosen[None, :, None], CAP, counts).astype(jnp.int32)


def draw_send_counts(key, part):
    return shared_counts(key)


def draw_neighbors(key, part):
    counts = shared_counts(key)
    spaces = NZ // CZ
    shape = (NZ, NX // 4, NY // 4, SLOTS)
    source = jax.random.randint(jax.random.fold_in(key, 21), shape, 0, spaces)
    drawn = jax.random.randint(jax.random.fold_in(key, 22), shape, 0, 1 << 20)
    owner = jnp.broadcast_to((jnp.arange(NZ) // CZ)[:, None, None, None], shape)
    column = jnp.broadcast_to((jnp.arange(NX // 4) // (CX // 4))[None, :, None, None], shape)
    limit = counts[source, column, owner]
    return (source * CAP + drawn % limit).astype(jnp.int32)


def plant(entries, stream_key, low, top_value):
    shape = entries.shape
    spot = [jax.random.randint(jax.random.fold_in(stream_key, axis), (), 0, shape[axis]) for axis in range(len(shape))]
    entries = entries.at[tuple(spot)].set(low)
    longest = shape.index(max(shape))
    spot[longest] = (spot[longest] + 1) % shape[longest]
    return entries.at[tuple(spot)].set(top_value)


def shard_levels(rng, extent, pieces, least, largest):
    level = 1.0
    for axis_at, shards_of in pieces:
        draws = jax.random.uniform(jax.random.fold_in(jax.random.fold_in(rng, 6), axis_at), (shards_of,), jnp.float32, least / len(pieces), largest / len(pieces))
        level = level * jnp.repeat(jnp.exp(draws), extent[axis_at] // shards_of).reshape((-1,) + (1,) * (len(extent) - 1 - axis_at))
    return level


def noise(own_key, dims, scale, reach, shards=(), held_as=jnp.bfloat16):
    gain = shard_levels(own_key, dims, shards, -0.22, 0.18) if shards else 1.0
    values = jax.random.normal(own_key, dims, jnp.float32) * scale * gain
    return jnp.minimum(jnp.maximum(values, -reach), reach).astype(held_as)


def setup_inputs(seed: int = 0) -> dict:
    seeds = jax.random.split(jax.random.key(seed), 10)
    point_feats = noise(seeds[0], (NPTS, C), 1.0, 6.0, ((0, 128),))
    send_slots = plant(jax.random.randint(seeds[1], (N_SPACE, N_CHAN, N_SPACE, CAP), 0, PTS_DEV), jax.random.fold_in(seeds[1], 1), 0, PTS_DEV - 1).astype(jnp.int32)
    send_counts = draw_send_counts(jax.random.fold_in(seeds[9], 71), 0)
    neighbors = draw_neighbors(jax.random.fold_in(seeds[9], 71), 0)
    tile_fill = plant(jax.random.randint(seeds[4], (NZ, NX // 4, NY // 4), 16, SLOTS + 1), jax.random.fold_in(seeds[4], 1), 16, SLOTS).astype(jnp.int32)
    offsets = jnp.clip(jax.random.uniform(seeds[5], (NZ, NX // 4, NY // 4, 3, SLOTS), jnp.float32, -2.5, 2.5) * shard_levels(seeds[5], (NZ, NX // 4, NY // 4, 3, SLOTS), ((0, 4), (1, 32)), -0.4, 0.0), -2.5, 2.5)
    weight = noise(seeds[6], (C, 27, C), (27 * C) ** -0.5, 0.078125, ((0, 32),))
    conv_bias = noise(seeds[7], (C,), 0.5, 3.0)
    cotangent = noise(seeds[8], (NZ, NX, NY, C), 1.0, 6.0, ((0, 4), (1, 32)))
    return {"point_feats": point_feats, "send_slots": send_slots, "send_counts": send_counts, "neighbors": neighbors, "tile_fill": tile_fill, "offsets": offsets, "weight": weight, "conv_bias": conv_bias, "cotangent": cotangent}


def kernel_weights(offsets, fill_count):
    centres = jnp.arange(4, dtype=jnp.float32) - 1.5
    along_x = offsets[..., 0, :][..., None, None, :] - centres[:, None, None]
    along_y = offsets[..., 1, :][..., None, None, :] - centres[None, :, None]
    along_z = offsets[..., 2, :][..., None, None, :]
    values = jnp.exp(-0.5 * (along_x * along_x + along_y * along_y + along_z * along_z))
    in_use = jnp.arange(offsets.shape[-1], dtype=jnp.int32) < fill_count[..., None]
    return jnp.where(in_use[..., None, None, :], values, jnp.zeros((), values.dtype))

def conv_whole(padded, weight):
    planes = padded.shape[0] - 2
    width_x = padded.shape[1] - 2
    width_y = padded.shape[2] - 2
    weight_wide = weight.astype(jnp.float32)
    running = jnp.zeros((planes, width_x, width_y, weight.shape[2]), jnp.float32)
    for position in range(27):
        shift_z, shift_x, shift_y = (position // 9, position // 3 % 3, position % 3)
        window = padded[shift_z:shift_z + planes, shift_x:shift_x + width_x, shift_y:shift_y + width_y, :].astype(jnp.float32)
        running = running + jnp.einsum('zxyi,io->zxyo', window, weight_wide[:, position, :])
    return running

def grad_whole(padded, grad_pre):
    planes = padded.shape[0] - 2
    width_x = padded.shape[1] - 2
    width_y = padded.shape[2] - 2
    grad_wide = grad_pre.astype(jnp.float32)
    term_list = []
    for position in range(27):
        shift_z, shift_x, shift_y = (position // 9, position // 3 % 3, position % 3)
        window = padded[shift_z:shift_z + planes, shift_x:shift_x + width_x, shift_y:shift_y + width_y, :].astype(jnp.float32)
        term_list.append(jnp.einsum('zxyi,zxyo->io', window, grad_wide))
    return jnp.stack(term_list, 1)

def reference(point_feats, send_slots, send_counts, neighbors, tile_fill, offsets, weight, conv_bias, cotangent):
    spaces = send_counts.shape[0]
    chans = send_counts.shape[1]
    points = point_feats.reshape(spaces, chans, PTS_DEV, C)
    space_ids = jnp.arange(spaces, dtype=jnp.int32)[:, None, None, None]
    chan_ids = jnp.arange(chans, dtype=jnp.int32)[None, :, None, None]
    gathered_rows = points[space_ids, chan_ids, send_slots]
    usable = jnp.arange(CAP, dtype=jnp.int32)[None, None, None, :] < send_counts[..., None]
    gathered_rows = jnp.where(usable[..., None], gathered_rows, jnp.zeros((), jnp.bfloat16))
    received = gathered_rows.transpose(2, 1, 0, 3, 4).reshape(spaces, chans, spaces * CAP, C)
    tile_owner = (jnp.arange(NX // 4, dtype=jnp.int32) // (CX // 4)).astype(jnp.int32)

    def encode_plane(items):
        plane_index, near_rows, fill_count, place_offsets = items
        owner_index = (plane_index // CZ).astype(jnp.int32)
        point_table = lax.dynamic_index_in_dim(received, owner_index, 0, keepdims=False)
        picked = point_table[tile_owner[:, None, None], near_rows].astype(jnp.float32)
        kernel = kernel_weights(place_offsets, fill_count)
        denominator = 1.0 + lax.optimization_barrier(jnp.sum(kernel, axis=-1))
        kernel_half = kernel.astype(jnp.bfloat16).astype(jnp.float32)
        summed = jnp.einsum('abuvs,absk->abuvk', kernel_half, picked)
        tile_sums = (summed / denominator[..., None]).astype(jnp.bfloat16)
        return tile_sums.transpose(0, 2, 1, 3, 4).reshape(NX, NY, C)
    latent = lax.map(encode_plane, (jnp.arange(NZ, dtype=jnp.int32), neighbors, tile_fill, offsets))
    padded = jnp.pad(latent, ((1, 1), (1, 1), (1, 1), (0, 0)))
    pre_act = conv_whole(padded, weight) + conv_bias.astype(jnp.float32)
    activated = jax.nn.gelu(pre_act).astype(jnp.bfloat16)
    _, backward = jax.vjp(jax.nn.gelu, pre_act)
    grad_pre = backward(cotangent.astype(pre_act.dtype))[0].astype(jnp.bfloat16)
    weight_grad = grad_whole(padded, grad_pre) * (1.0 / math.sqrt(NZ * NX * NY))
    return (activated, weight_grad)
```

```python
import math

import jax
import jax.numpy as jnp
from jax import lax
from jax.experimental import pallas as pl
from jax.experimental.pallas import tpu as pltpu
from jax.sharding import PartitionSpec as P

BF = jnp.bfloat16
F32 = jnp.float32


def send_kernel(slots_ref, counts_ref, feats_ref, out_ref):
    owner = pl.program_id(0)
    points = feats_ref.shape[0]
    slots = slots_ref[0]
    position = lax.broadcasted_iota(jnp.int32, slots.shape, 0) * 128 + lax.broadcasted_iota(
        jnp.int32, slots.shape, 1
    )
    slots = jnp.where(position < counts_ref[owner], slots, -1)
    columns = slots.T
    point_ids = lax.broadcasted_iota(jnp.int32, (128, points), 1)
    for half in range(2):
        hot = [
            jnp.where(point_ids == columns[:, r : r + 1], 1.0, 0.0).astype(BF)
            for r in range(half * 4, half * 4 + 4)
        ]
        rows = jnp.dot(
            jnp.concatenate(hot, axis=0), feats_ref[...], preferred_element_type=F32
        )
        out_ref[0, half * 512 : half * 512 + 512, :] = rows.astype(BF)


def gather_listed(feats, slots, counts):
    owners, capacity = slots.shape
    points, channels = feats.shape
    return pl.pallas_call(
        send_kernel,
        grid=(owners,),
        in_specs=[
            pl.BlockSpec((1, capacity // 128, 128), lambda t: (t, 0, 0)),
            pl.BlockSpec(memory_space=pltpu.SMEM),
            pl.BlockSpec((points, channels), lambda t: (0, 0)),
        ],
        out_specs=pl.BlockSpec((1, capacity, channels), lambda t: (t, 0, 0)),
        out_shape=jax.ShapeDtypeStruct((owners, capacity, channels), BF),
        compiler_params=pltpu.CompilerParams(vmem_limit_bytes=40 << 20),
    )(slots.reshape(owners, capacity // 128, 128), counts, feats)


def latent_kernel(fill_ref, near_ref, place_ref, table_ref, out_ref, spread, total, order, denom):
    plane = pl.program_id(0)
    tiles = near_ref.shape[1]
    slots = near_ref.shape[2]
    rows = table_ref.shape[0]
    channels = table_ref.shape[1]
    groups = rows // 256
    cell = lax.broadcasted_iota(jnp.int32, (16, slots), 0)
    centre_x = (cell // 4).astype(F32) - 1.5
    centre_y = (cell % 4).astype(F32) - 1.5
    lane = lax.broadcasted_iota(jnp.int32, (16, slots), 1)
    low_ids = lax.broadcasted_iota(jnp.int32, (256, slots), 0)

    def one_tile(tile, carry):
        near = near_ref[0, pl.ds(tile, 1), :]
        along_x = place_ref[0, 0, pl.ds(tile, 1), :] - centre_x
        along_y = place_ref[0, 1, pl.ds(tile, 1), :] - centre_y
        along_z = place_ref[0, 2, pl.ds(tile, 1), :]
        values = jnp.exp(-0.5 * (along_x * along_x + along_y * along_y + along_z * along_z))
        values = jnp.where(lane < fill_ref[plane, tile], values, 0.0)
        start = pl.multiple_of(tile * 16, 16)
        denom[pl.ds(start, 16), :] = 1.0 + jnp.sum(values, axis=1, keepdims=True)
        half = values.astype(BF).astype(F32)
        high = jnp.broadcast_to(near >> 8, (16, slots))
        low = near & 255
        stacked = jnp.concatenate(
            [jnp.where(high == g, half, 0.0).astype(BF) for g in range(groups)], axis=0
        )
        hot = jnp.where(low_ids == low, 1.0, 0.0).astype(BF)
        block = lax.dot_general(
            stacked, hot, (((1,), (1,)), ((), ())), preferred_element_type=F32
        ).astype(BF)
        for g in range(groups):
            spread[pl.ds(start, 16), g * 256 : g * 256 + 256] = block[g * 16 : g * 16 + 16, :]
        return carry

    lax.fori_loop(0, tiles, one_tile, 0, unroll=4)
    summed = jnp.dot(spread[...], table_ref[...], preferred_element_type=F32)
    summed = summed / denom[...]
    for lanes in range(0, channels, 128):
        total[...] = summed[:, lanes : lanes + 128]
        for u in range(4):
            for v in range(4):
                order[pl.ds(v, tiles, stride=4), :] = total[
                    pl.ds(u * 4 + v, tiles, stride=16), :
                ]
            out_ref[0, u, :, lanes : lanes + 128] = order[...].astype(BF)


def latent_block(table, near, fill, place):
    planes, tiles, slots = near.shape
    rows, channels = table.shape
    return pl.pallas_call(
        latent_kernel,
        grid=(planes,),
        in_specs=[
            pl.BlockSpec(memory_space=pltpu.SMEM),
            pl.BlockSpec((1, tiles, slots), lambda z: (z, 0, 0)),
            pl.BlockSpec((1, 3, tiles, slots), lambda z: (z, 0, 0, 0)),
            pl.BlockSpec((rows, channels), lambda z: (0, 0)),
        ],
        out_specs=pl.BlockSpec((1, 4, tiles * 4, channels), lambda z: (z, 0, 0, 0)),
        out_shape=jax.ShapeDtypeStruct((planes, 4, tiles * 4, channels), BF),
        scratch_shapes=[
            pltpu.VMEM((tiles * 16, rows), BF),
            pltpu.VMEM((tiles * 16, 128), F32),
            pltpu.VMEM((tiles * 4, 128), F32),
            pltpu.VMEM((tiles * 16, 1), F32),
        ],
        compiler_params=pltpu.CompilerParams(vmem_limit_bytes=40 << 20),
    )(fill, near, place, table)


def conv_kernel(
    latent_ref, below_ref, above_ref, left_ref, right_ref, left_rim_ref, right_rim_ref,
    weight_ref, bias_ref, cotangent_ref, act_ref, grad_ref, padded, turned, taps, shifted,
):
    planes, rows_x, width, channels = latent_ref.shape
    flat = rows_x * width
    padded[1 : planes + 1, 1 : rows_x + 1] = latent_ref[...]
    padded[0:1, 1 : rows_x + 1] = below_ref[...]
    padded[planes + 1 : planes + 2, 1 : rows_x + 1] = above_ref[...]
    padded[1 : planes + 1, 0:1] = left_ref[...]
    padded[1 : planes + 1, rows_x + 1 : rows_x + 2] = right_ref[...]
    for rim in range(2):
        z = rim * (planes + 1)
        padded[z : z + 1, 0:1] = left_rim_ref[rim : rim + 1]
        padded[z : z + 1, rows_x + 1 : rows_x + 2] = right_rim_ref[rim : rim + 1]
    y_ids = lax.broadcasted_iota(jnp.int32, (width, channels), 0)
    root = math.sqrt(2.0 / math.pi)

    def turn(z, carry):
        block = padded[z].reshape((rows_x + 2) * width, channels)
        turned[z] = block.T
        return carry

    lax.fori_loop(0, planes + 2, turn, 0)

    def conv_plane(z, carry):
        pieces = [
            padded[z + dz, dx : dx + rows_x].reshape(flat, channels)
            for dz in range(3)
            for dx in range(3)
        ]
        taps[...] = jnp.dot(
            jnp.concatenate(pieces, axis=1), weight_ref[...], preferred_element_type=F32
        )
        for x in range(rows_x):
            rows = slice(x * width, (x + 1) * width)
            low = jnp.where(y_ids == 0, 0.0, pltpu.roll(taps[rows, 0:channels], 1, 0))
            high = jnp.where(
                y_ids == width - 1, 0.0, pltpu.roll(taps[rows, 2 * channels :], width - 1, 0)
            )
            pre = low + taps[rows, channels : 2 * channels] + high + bias_ref[...]
            square = pre * pre
            inner = root * (pre + 0.044715 * (square * pre))
            bent = jnp.tanh(inner)
            gate = 0.5 * (1.0 + bent)
            act_ref[z, x] = (pre * gate).astype(BF)
            slope = gate + 0.5 * pre * (1.0 - bent * bent) * (
                root * (1.0 + 3.0 * 0.044715 * square)
            )
            grad = (cotangent_ref[z, x].astype(F32) * slope).astype(BF).astype(F32)
            start = pl.multiple_of(z * flat + x * width, width)
            shifted[pl.ds(start, width), 0:channels] = jnp.where(
                y_ids == width - 1, 0.0, pltpu.roll(grad, width - 1, 0)
            ).astype(BF)
            shifted[pl.ds(start, width), channels : 2 * channels] = grad.astype(BF)
            shifted[pl.ds(start, width), 2 * channels :] = jnp.where(
                y_ids == 0, 0.0, pltpu.roll(grad, 1, 0)
            ).astype(BF)
        return carry

    lax.fori_loop(0, planes, conv_plane, 0)

    def grad_taps(tap, carry):
        dz = tap // 3
        start = pl.multiple_of((tap % 3) * width, width)
        pieces = [turned[z + dz, :, pl.ds(start, flat)] for z in range(planes)]
        sums = jnp.dot(
            jnp.concatenate(pieces, axis=1), shifted[...], preferred_element_type=F32
        )
        for dy in range(3):
            part = sums[:, dy * channels : (dy + 1) * channels]
            both = jnp.concatenate(
                [
                    part[:, :128].reshape(channels // 8, 8, 128),
                    part[:, 128:].reshape(channels // 8, 8, 128),
                ],
                axis=1,
            )
            grad_ref[:, tap * 3 + dy] = both.astype(BF)
        return carry

    lax.fori_loop(0, 9, grad_taps, 0)


def conv_block(
    latent, below, above, left, right, left_rim, right_rim, weight, bias, cotangent
):
    planes, rows_x, width, channels = latent.shape
    flat = rows_x * width
    whole = pl.BlockSpec(memory_space=pltpu.VMEM)
    return pl.pallas_call(
        conv_kernel,
        in_specs=[whole] * 10,
        out_specs=[whole] * 2,
        out_shape=[
            jax.ShapeDtypeStruct(latent.shape, BF),
            jax.ShapeDtypeStruct((channels // 8, 27, 16, 128), BF),
        ],
        scratch_shapes=[
            pltpu.VMEM((planes + 2, rows_x + 2, width, channels), BF),
            pltpu.VMEM((planes + 2, channels, (rows_x + 2) * width), BF),
            pltpu.VMEM((flat, 3 * channels), F32),
            pltpu.VMEM((planes * flat, 3 * channels), BF),
        ],
        compiler_params=pltpu.CompilerParams(vmem_limit_bytes=52 << 20),
    )(latent, below, above, left, right, left_rim, right_rim, weight, bias, cotangent)


def in_order(core, own, other):
    low = jnp.where(core == 0, own, other)
    high = jnp.where(core == 0, other, own)
    return low, high


def on_device(
    point_feats,
    send_slots,
    send_counts,
    neighbors,
    tile_fill,
    offsets,
    weight,
    conv_bias,
    cotangent,
):
    spaces = lax.axis_size("space")
    chans = lax.axis_size("chan")
    planes, rows_x, width_y, channels = cotangent.shape
    row_count = weight.shape[0]
    space = lax.axis_index("space")
    core = space % 2
    swap = [(i, i ^ 1) for i in range(spaces)]
    far = [(i, i ^ 2) for i in range(spaces)]
    cross = [(i, i ^ 3) for i in range(spaces)]
    up_space = [(i, i + 1) for i in range(spaces - 1)]
    down_space = [(i + 1, i) for i in range(spaces - 1)]
    up_chan = [(i, i + 1) for i in range(chans - 1)]
    down_chan = [(i + 1, i) for i in range(chans - 1)]

    by_tap = weight.transpose(1, 0, 2)
    half_taps = lax.dynamic_slice_in_dim(by_tap, core * 13, 14, 0)
    spread = jnp.broadcast_to(half_taps[None], (chans,) + half_taps.shape)
    gathered = lax.all_to_all(spread, "chan", split_axis=0, concat_axis=0, tiled=True)
    gathered_other = lax.ppermute(gathered, "space", swap)
    low, high = in_order(core, gathered, gathered_other)
    full_weight = jnp.concatenate([low, high[:, 1:]], axis=1)
    full_weight = full_weight.reshape(chans, 9, 3, row_count, channels)
    full_weight = full_weight.transpose(1, 0, 3, 2, 4).reshape(9 * channels, 3 * channels)

    outgoing = gather_listed(point_feats, send_slots[0, 0], send_counts[0, 0])
    incoming = lax.all_to_all(outgoing, "space", split_axis=0, concat_axis=0, tiled=True)
    table = incoming.reshape(-1, channels)
    latent = latent_block(
        table, neighbors[:, 0], tile_fill[:, 0], offsets[:, 0].transpose(0, 2, 1, 3)
    )

    below = lax.ppermute(latent[planes - 1 :], "space", up_space)
    above = lax.ppermute(latent[:1], "space", down_space)
    left = lax.ppermute(latent[:, rows_x - 1 :], "chan", up_chan)
    right = lax.ppermute(latent[:, :1], "chan", down_chan)
    rims = jnp.concatenate([below, above], axis=0)
    left_rim = lax.ppermute(rims[:, rows_x - 1 :], "chan", up_chan)
    right_rim = lax.ppermute(rims[:, :1], "chan", down_chan)
    activated, terms = conv_block(
        latent, below, above, left, right, left_rim, right_rim,
        full_weight, conv_bias.astype(F32)[None], cotangent,
    )

    mine = lax.dynamic_slice_in_dim(terms, core * 13, 14, 1)
    theirs = lax.dynamic_slice_in_dim(terms, (1 - core) * 13, 14, 1)
    paired = (mine.astype(F32) + lax.ppermute(theirs, "space", swap).astype(F32)).astype(BF)
    collected = lax.all_to_all(paired, "chan", split_axis=0, concat_axis=0, tiled=True)
    summed = jnp.sum(collected.astype(F32), axis=0)
    own_sum = summed + lax.ppermute(summed, "space", far)
    other_sum = lax.ppermute(summed, "space", swap) + lax.ppermute(summed, "space", cross)
    low_sum, high_sum = in_order(core, own_sum, other_sum)
    total = jnp.concatenate([low_sum, high_sum[1:]], axis=0)
    total = total.reshape(27, 2, row_count, channels // 2).transpose(2, 0, 1, 3)
    scaling = 1.0 / math.sqrt(planes * spaces * rows_x * chans * width_y)
    return (activated, total.reshape(row_count, 27, channels) * scaling)


def solution(mesh):
    return jax.shard_map(
        on_device,
        mesh=mesh,
        in_specs=(
            P(("space", "chan"), None),
            P("space", "chan", None, None),
            P("space", "chan", None),
            P("space", "chan", None, None),
            P("space", "chan", None),
            P("space", "chan", None, None, None),
            P("chan", None, None),
            P(),
            P("space", "chan", None, None),
        ),
        out_specs=(P("space", "chan", None, None), P("chan", None, None)),
        check_vma=False,
    )
```

```python
import math

import jax
import jax.numpy as jnp
from jax import lax
from jax.experimental import pallas as pl
from jax.experimental.pallas import tpu as pltpu
from jax.sharding import PartitionSpec as P

BF = jnp.bfloat16
F32 = jnp.float32


def send_kernel(owner_ref, slots_ref, counts_ref, feats_ref, *out_refs):
    points = feats_ref.shape[0]
    point_ids = lax.broadcasted_iota(jnp.int32, (128, points), 1)
    for place, out_ref in enumerate(out_refs):
        owner = owner_ref[place]
        slots = slots_ref[owner]
        position = lax.broadcasted_iota(
            jnp.int32, slots.shape, 0
        ) * 128 + lax.broadcasted_iota(jnp.int32, slots.shape, 1)
        columns = jnp.where(position < counts_ref[owner], slots, -1).T
        for half in range(2):
            hot = [
                jnp.where(point_ids == columns[:, r : r + 1], 1.0, 0.0).astype(BF)
                for r in range(half * 4, half * 4 + 4)
            ]
            rows = jnp.dot(
                jnp.concatenate(hot, axis=0), feats_ref[...], preferred_element_type=F32
            )
            out_ref[half * 512 : half * 512 + 512, :] = rows.astype(BF)


def gather_listed(feats, slots, counts, owners):
    spaces, capacity = slots.shape
    channels = feats.shape[1]
    whole = pl.BlockSpec(memory_space=pltpu.VMEM)
    scalars = pl.BlockSpec(memory_space=pltpu.SMEM)
    count = owners.shape[0]
    return pl.pallas_call(
        send_kernel,
        in_specs=[scalars, whole, scalars, whole],
        out_specs=[whole] * count,
        out_shape=[jax.ShapeDtypeStruct((capacity, channels), BF)] * count,
        compiler_params=pltpu.CompilerParams(vmem_limit_bytes=40 << 20),
    )(owners, slots.reshape(spaces, capacity // 128, 128), counts, feats)


def spread_kernel(fill_ref, near_ref, place_ref, out_ref, denom_ref):
    plane = pl.program_id(0)
    tiles = near_ref.shape[1]
    slots = near_ref.shape[2]
    groups = out_ref.shape[1] // 256
    cell = lax.broadcasted_iota(jnp.int32, (16, slots), 0)
    centre_x = (cell // 4).astype(F32) - 1.5
    centre_y = (cell % 4).astype(F32) - 1.5
    lane = lax.broadcasted_iota(jnp.int32, (16, slots), 1)
    low_ids = lax.broadcasted_iota(jnp.int32, (256, slots), 0)

    def one_tile(tile, carry):
        near = near_ref[0, pl.ds(tile, 1), :]
        along_x = place_ref[0, 0, pl.ds(tile, 1), :] - centre_x
        along_y = place_ref[0, 1, pl.ds(tile, 1), :] - centre_y
        along_z = place_ref[0, 2, pl.ds(tile, 1), :]
        values = jnp.exp(-0.5 * (along_x * along_x + along_y * along_y + along_z * along_z))
        values = jnp.where(lane < fill_ref[plane, tile], values, 0.0)
        start = pl.multiple_of(tile * 16, 16)
        denom_ref[pl.ds(start, 16), :] = jnp.broadcast_to(
            1.0 + jnp.sum(values, axis=1, keepdims=True), (16, 128)
        )
        half = values.astype(BF).astype(F32)
        high = jnp.broadcast_to(near >> 8, (16, slots))
        low = near & 255
        stacked = jnp.concatenate(
            [jnp.where(high == g, half, 0.0).astype(BF) for g in range(groups)], axis=0
        )
        hot = jnp.where(low_ids == low, 1.0, 0.0).astype(BF)
        block = lax.dot_general(
            stacked, hot, (((1,), (1,)), ((), ())), preferred_element_type=F32
        ).astype(BF)
        for g in range(groups):
            out_ref[pl.ds(start, 16), g * 256 : g * 256 + 256] = block[g * 16 : g * 16 + 16, :]
        return carry

    lax.fori_loop(0, tiles, one_tile, 0, unroll=4)


def spread_weights(near, fill, place, rows):
    planes, tiles, slots = near.shape
    return pl.pallas_call(
        spread_kernel,
        grid=(planes,),
        in_specs=[
            pl.BlockSpec(memory_space=pltpu.SMEM),
            pl.BlockSpec((1, tiles, slots), lambda z: (z, 0, 0)),
            pl.BlockSpec((1, 3, tiles, slots), lambda z: (z, 0, 0, 0)),
        ],
        out_specs=[
            pl.BlockSpec((tiles * 16, rows), lambda z: (z, 0)),
            pl.BlockSpec((tiles * 16, 128), lambda z: (z, 0)),
        ],
        out_shape=[
            jax.ShapeDtypeStruct((planes * tiles * 16, rows), BF),
            jax.ShapeDtypeStruct((planes * tiles * 16, 128), F32),
        ],
        compiler_params=pltpu.CompilerParams(vmem_limit_bytes=40 << 20),
        cost_estimate=pl.CostEstimate(
            flops=4 << 30, bytes_accessed=18 << 20, transcendentals=1 << 20
        ),
    )(fill, near, place)


def latent_kernel(
    flags_ref, spread_ref, denom_ref, t0, t1, t2, t3,
    out_ref, near_ref, far_ref, low_ref, high_ref, total, order,
):
    plane = pl.program_id(0)
    last = pl.num_programs(0) - 1
    core = flags_ref[0]
    capacity, channels = t0.shape
    cells = spread_ref.shape[0]
    tiles = cells // 16
    summed = jnp.dot(
        spread_ref[:, 0:capacity], t0[...], preferred_element_type=F32
    )
    for place, table in ((1, t1), (2, t2), (3, t3)):
        summed = summed + jnp.dot(
            spread_ref[:, place * capacity : (place + 1) * capacity],
            table[...],
            preferred_element_type=F32,
        )
    for lanes in range(0, channels, 128):
        part = slice(lanes, lanes + 128)
        total[...] = summed[:, part] / denom_ref[...]
        for u in range(4):
            for v in range(4):
                order[pl.ds(v, tiles, stride=4), :] = total[
                    pl.ds(u * 4 + v, tiles, stride=16), :
                ]
            out_ref[0, u, :, part] = order[...].astype(BF)
    low_ref[0, 0] = out_ref[0, 0]
    high_ref[0, 0] = out_ref[0, 3]

    @pl.when(plane == (1 - core) * last)
    def _():
        near_ref[...] = out_ref[...]

    @pl.when(plane == core * last)
    def _():
        far_ref[...] = out_ref[...]


def latent_block(flags, spread, denom, tables):
    cells = spread.shape[0]
    planes = 4
    per_plane = cells // planes
    capacity, channels = tables[0].shape
    width = per_plane // 4
    whole = pl.BlockSpec((capacity, channels), lambda z: (0, 0))
    plane_spec = pl.BlockSpec((1, 4, width, channels), lambda z: (0, 0, 0, 0))
    row_spec = pl.BlockSpec((1, 1, width, channels), lambda z: (z, 0, 0, 0))
    return pl.pallas_call(
        latent_kernel,
        grid=(planes,),
        in_specs=[
            pl.BlockSpec(memory_space=pltpu.SMEM),
            pl.BlockSpec((per_plane, spread.shape[1]), lambda z: (z, 0)),
            pl.BlockSpec((per_plane, 128), lambda z: (z, 0)),
        ]
        + [whole] * 4,
        out_specs=[
            pl.BlockSpec((1, 4, width, channels), lambda z: (z, 0, 0, 0)),
            plane_spec,
            plane_spec,
            row_spec,
            row_spec,
        ],
        out_shape=[
            jax.ShapeDtypeStruct((planes, 4, width, channels), BF),
            jax.ShapeDtypeStruct((1, 4, width, channels), BF),
            jax.ShapeDtypeStruct((1, 4, width, channels), BF),
            jax.ShapeDtypeStruct((planes, 1, width, channels), BF),
            jax.ShapeDtypeStruct((planes, 1, width, channels), BF),
        ],
        scratch_shapes=[
            pltpu.VMEM((per_plane, 128), F32),
            pltpu.VMEM((width, 128), F32),
        ],
        compiler_params=pltpu.CompilerParams(vmem_limit_bytes=40 << 20),
    )(flags, spread, denom, *tables)


def conv_kernel(
    flags_ref, latent_ref, near_ref, far_ref, left_ref, right_ref, left_rim_ref, right_rim_ref,
    weight_ref, bias_ref, cotangent_ref, act_ref, keep_ref, give_ref,
    padded, turned, taps, shifted,
):
    planes, rows_x, width, channels = latent_ref.shape
    flat = rows_x * width
    padded[1 : planes + 1, 1 : rows_x + 1] = latent_ref[...]
    core = flags_ref[0]
    has_far = flags_ref[1] > 0
    has_left = flags_ref[2] > 0
    has_right = flags_ref[3] > 0
    near_z = (1 - core) * (planes + 1)
    far_z = core * (planes + 1)
    none = jnp.zeros((), BF)
    padded[pl.ds(near_z, 1), 1 : rows_x + 1] = near_ref[...]
    padded[pl.ds(far_z, 1), 1 : rows_x + 1] = jnp.where(has_far, far_ref[...], none)
    for has, column, face_ref, rim_ref in (
        (has_left, 0, left_ref, left_rim_ref),
        (has_right, rows_x + 1, right_ref, right_rim_ref),
    ):
        padded[1 : planes + 1, column] = jnp.where(has, face_ref[:, 0], none)
        padded[pl.ds(near_z, 1), column] = jnp.where(has, rim_ref[0:1], none)
        padded[pl.ds(far_z, 1), column] = jnp.where(
            jnp.logical_and(has, has_far), rim_ref[1:2], none
        )
    y_ids = lax.broadcasted_iota(jnp.int32, (width, channels), 0)
    root = math.sqrt(2.0 / math.pi)

    def turn(z, carry):
        block = padded[z].reshape((rows_x + 2) * width, channels)
        turned[z] = block.T
        return carry

    lax.fori_loop(0, planes + 2, turn, 0)

    def conv_plane(z, carry):
        pieces = [
            padded[z + dz, dx : dx + rows_x].reshape(flat, channels)
            for dz in range(3)
            for dx in range(3)
        ]
        patch = jnp.concatenate(pieces, axis=1)
        for dy in range(3):
            matrix = jnp.concatenate([weight_ref[3 * tap + dy] for tap in range(9)], axis=0)
            taps[:, dy * channels : (dy + 1) * channels] = jnp.dot(
                patch, matrix, preferred_element_type=F32
            )
        for x in range(rows_x):
            rows = slice(x * width, (x + 1) * width)
            low = jnp.where(y_ids == 0, 0.0, pltpu.roll(taps[rows, 0:channels], 1, 0))
            high = jnp.where(
                y_ids == width - 1, 0.0, pltpu.roll(taps[rows, 2 * channels :], width - 1, 0)
            )
            pre = low + taps[rows, channels : 2 * channels] + high + bias_ref[...]
            square = pre * pre
            inner = root * (pre + 0.044715 * (square * pre))
            bent = jnp.tanh(inner)
            gate = 0.5 * (1.0 + bent)
            act_ref[z, x] = (pre * gate).astype(BF)
            slope = gate + 0.5 * pre * (1.0 - bent * bent) * (
                root * (1.0 + 3.0 * 0.044715 * square)
            )
            grad = (cotangent_ref[z, x].astype(F32) * slope).astype(BF).astype(F32)
            start = pl.multiple_of(z * flat + x * width, width)
            shifted[pl.ds(start, width), 0:channels] = jnp.where(
                y_ids == width - 1, 0.0, pltpu.roll(grad, width - 1, 0)
            ).astype(BF)
            shifted[pl.ds(start, width), channels : 2 * channels] = grad.astype(BF)
            shifted[pl.ds(start, width), 2 * channels :] = jnp.where(
                y_ids == 0, 0.0, pltpu.roll(grad, 1, 0)
            ).astype(BF)
        return carry

    lax.fori_loop(0, planes, conv_plane, 0)

    def grad_taps(tap, carry):
        dz = tap // 3
        start = pl.multiple_of((tap % 3) * width, width)
        pieces = [turned[z + dz, :, pl.ds(start, flat)] for z in range(planes)]
        sums = jnp.dot(
            jnp.concatenate(pieces, axis=1), shifted[...], preferred_element_type=F32
        )
        for dy in range(3):
            part = sums[:, dy * channels : (dy + 1) * channels]
            both = jnp.concatenate(
                [
                    part[:, :128].reshape(channels // 8, 8, 128),
                    part[:, 128:].reshape(channels // 8, 8, 128),
                ],
                axis=1,
            )
            position = tap * 3 + dy
            half = position // 14
            slot = position - half * 14
            rounded = both.astype(BF)

            @pl.when(half == core)
            def _():
                keep_ref[:, slot] = rounded

            @pl.when(half != core)
            def _():
                give_ref[:, slot] = rounded
        return carry

    lax.fori_loop(0, 9, grad_taps, 0)
    unused = jnp.zeros((channels // 8, 16, 128), BF)

    @pl.when(core == 1)
    def _():
        keep_ref[:, 13] = unused

    @pl.when(core == 0)
    def _():
        give_ref[:, 13] = unused


def conv_block(
    flags, latent, near, far, left, right, left_rim, right_rim, weight, bias, cotangent
):
    planes, rows_x, width, channels = latent.shape
    flat = rows_x * width
    whole = pl.BlockSpec(memory_space=pltpu.VMEM)
    half_terms = jax.ShapeDtypeStruct((channels // 8, 14, 16, 128), BF)
    return pl.pallas_call(
        conv_kernel,
        in_specs=[pl.BlockSpec(memory_space=pltpu.SMEM)] + [whole] * 10,
        out_specs=[whole] * 3,
        out_shape=[jax.ShapeDtypeStruct(latent.shape, BF), half_terms, half_terms],
        scratch_shapes=[
            pltpu.VMEM((planes + 2, rows_x + 2, width, channels), BF),
            pltpu.VMEM((planes + 2, channels, (rows_x + 2) * width), BF),
            pltpu.VMEM((flat, 3 * channels), F32),
            pltpu.VMEM((planes * flat, 3 * channels), BF),
        ],
        compiler_params=pltpu.CompilerParams(vmem_limit_bytes=52 << 20),
    )(flags, latent, near, far, left, right, left_rim, right_rim, weight, bias, cotangent)


def in_order(core, own, other):
    low = jnp.where(core == 0, own, other)
    high = jnp.where(core == 0, other, own)
    return low, high


def on_device(
    point_feats,
    send_slots,
    send_counts,
    neighbors,
    tile_fill,
    offsets,
    weight,
    conv_bias,
    cotangent,
):
    spaces = lax.axis_size("space")
    chans = lax.axis_size("chan")
    planes, rows_x, width_y, channels = cotangent.shape
    row_count = weight.shape[0]
    space = lax.axis_index("space")
    chan = lax.axis_index("chan")
    core = lax.rem(space, 2)
    swap = [(i, i ^ 1) for i in range(spaces)]
    far = [(i, i ^ 2) for i in range(spaces)]
    cross = [(i, i ^ 3) for i in range(spaces)]
    up_chan = [(i, (i + 1) % chans) for i in range(chans)]
    down_chan = [((i + 1) % chans, i) for i in range(chans)]
    flags = jnp.stack(
        [
            core,
            jnp.logical_or(space == 1, space == 2).astype(jnp.int32),
            (chan > 0).astype(jnp.int32),
            (chan < chans - 1).astype(jnp.int32),
        ]
    )

    slots, counts = send_slots[0, 0], send_counts[0, 0]
    owners = space ^ jnp.arange(spaces, dtype=jnp.int32)
    to_far, to_cross = gather_listed(point_feats, slots, counts, owners[2:])
    from_far = lax.ppermute(to_far, "space", far)
    from_cross = lax.ppermute(to_cross, "space", cross)
    held_feats, _ = lax.optimization_barrier((point_feats, to_far))
    to_self, to_other = gather_listed(held_feats, slots, counts, owners[:2])
    from_other = lax.ppermute(to_other, "space", swap)

    taps = jnp.pad(weight.transpose(1, 0, 2), ((0, 1), (0, 0), (0, 0)))
    gathered = lax.dynamic_slice_in_dim(taps, core * 14, 14, 0)
    for step, count in ((16, 2), (1, 4), (4, 4)):
        index = lax.rem(chan // step, count)
        pieces = [gathered] + [
            lax.ppermute(gathered, "chan", [(i, i ^ (offset * step)) for i in range(chans)])
            for offset in range(1, count)
        ]
        if step == 4:
            break
        gathered = jnp.zeros((count,) + gathered.shape, BF)
        for offset, piece in enumerate(pieces):
            gathered = lax.dynamic_update_index_in_dim(gathered, piece, index ^ offset, 0)
    gathered = jnp.zeros((2, count) + pieces[0].shape, BF)
    for offset, piece in enumerate(pieces):
        for half, part in ((core, piece), (1 - core, lax.ppermute(piece, "space", swap))):
            gathered = lax.dynamic_update_slice(
                gathered, part[None, None], (half, index ^ offset) + (0,) * part.ndim
            )
    full_weight = gathered.transpose(0, 4, 3, 1, 2, 5, 6).reshape(28, channels, channels)

    capacity = slots.shape[1]
    spread, denom = spread_weights(
        neighbors[:, 0] ^ (space * capacity),
        tile_fill[:, 0],
        offsets[:, 0].transpose(0, 2, 1, 3),
        spaces * capacity,
    )
    latent, near_plane, far_plane, low_row, high_row = latent_block(
        flags, spread, denom, (to_self, from_other, from_far, from_cross)
    )

    far_rim = lax.ppermute(far_plane, "space", cross)
    near_rim = lax.ppermute(near_plane, "space", swap)
    left = lax.ppermute(high_row, "chan", up_chan)
    right = lax.ppermute(low_row, "chan", down_chan)
    rims = jnp.concatenate([near_rim, far_rim], axis=0)
    left_rim = lax.ppermute(rims[:, rows_x - 1], "chan", up_chan)
    right_rim = lax.ppermute(rims[:, 0], "chan", down_chan)

    activated, keep, give = conv_block(
        flags, latent, near_rim, far_rim, left, right, left_rim, right_rim,
        full_weight, conv_bias.astype(F32)[None], cotangent,
    )

    paired = (keep.astype(F32) + lax.ppermute(give, "space", swap).astype(F32)).astype(BF)
    collected = lax.all_to_all(paired, "chan", split_axis=0, concat_axis=0, tiled=True)
    summed = jnp.sum(collected.astype(F32), axis=0)
    own_sum = summed + lax.ppermute(summed, "space", far)
    low_sum, high_sum = in_order(core, own_sum, lax.ppermute(own_sum, "space", swap))
    total = jnp.concatenate([low_sum, high_sum[:13]], axis=0)
    total = total.reshape(27, 2, row_count, channels // 2).transpose(2, 0, 1, 3)
    scaling = 1.0 / math.sqrt(planes * spaces * rows_x * chans * width_y)
    return (activated, total.reshape(row_count, 27, channels) * scaling)


def solution(mesh):
    return jax.shard_map(
        on_device,
        mesh=mesh,
        in_specs=(
            P(("space", "chan"), None),
            P("space", "chan", None, None),
            P("space", "chan", None),
            P("space", "chan", None, None),
            P("space", "chan", None),
            P("space", "chan", None, None, None),
            P("chan", None, None),
            P(),
            P("space", "chan", None, None),
        ),
        out_specs=(P("space", "chan", None, None), P("chan", None, None)),
        check_vma=False,
    )
```

```python
import functools
import math

import jax
import jax.numpy as jnp
from jax import lax
from jax.experimental import pallas as pl
from jax.experimental.pallas import tpu as pltpu
from jax.sharding import PartitionSpec as P

BF = jnp.bfloat16
F32 = jnp.float32
BRIEF = pl.CostEstimate(flops=1, bytes_accessed=1, transcendentals=0)


def send_kernel(scalars_ref, slots_ref, feats_ref, *out_refs):
    points = feats_ref.shape[0]
    point_ids = lax.broadcasted_iota(jnp.int32, (128, points), 1)
    for place, out_ref in enumerate(out_refs):
        owner = scalars_ref[place]
        slots = slots_ref[owner]
        position = lax.broadcasted_iota(
            jnp.int32, slots.shape, 0
        ) * 128 + lax.broadcasted_iota(jnp.int32, slots.shape, 1)
        columns = jnp.where(position < scalars_ref[2 + place], slots, -1).T
        for half in range(2):
            hot = [
                jnp.where(point_ids == columns[:, r : r + 1], 1.0, 0.0).astype(BF)
                for r in range(half * 4, half * 4 + 4)
            ]
            rows = jnp.dot(
                jnp.concatenate(hot, axis=0), feats_ref[...], preferred_element_type=F32
            )
            out_ref[half * 512 : half * 512 + 512, :] = rows.astype(BF)


def gather_listed(feats, slots, scalars):
    capacity = slots.shape[1] * slots.shape[2]
    channels = feats.shape[1]
    whole = pl.BlockSpec(memory_space=pltpu.VMEM)
    return pl.pallas_call(
        send_kernel,
        in_specs=[pl.BlockSpec(memory_space=pltpu.SMEM), whole, whole],
        out_specs=[whole] * 2,
        out_shape=[jax.ShapeDtypeStruct((capacity, channels), BF)] * 2,
        compiler_params=pltpu.CompilerParams(vmem_limit_bytes=16 << 20),
        cost_estimate=BRIEF,
    )(scalars, slots, feats)


def spread_kernel(fill_ref, near_ref, place_ref, t0, t1, out_ref, part_ref, denom_ref, close):
    plane = pl.program_id(0)
    tiles = near_ref.shape[1]
    slots = near_ref.shape[2]
    groups = (out_ref.shape[1] + close.shape[1]) // 256
    split = close.shape[1]
    capacity = t0.shape[0]
    cell = lax.broadcasted_iota(jnp.int32, (16, slots), 0)
    centre_x = (cell // 4).astype(F32) - 1.5
    centre_y = (cell % 4).astype(F32) - 1.5
    lane = lax.broadcasted_iota(jnp.int32, (16, slots), 1)
    low_ids = lax.broadcasted_iota(jnp.int32, (256, slots), 0)

    def one_tile(tile, carry):
        near = near_ref[0, pl.ds(tile, 1), :]
        along_x = place_ref[0, 0, pl.ds(tile, 1), :] - centre_x
        along_y = place_ref[0, 1, pl.ds(tile, 1), :] - centre_y
        along_z = place_ref[0, 2, pl.ds(tile, 1), :]
        values = jnp.exp(-0.5 * (along_x * along_x + along_y * along_y + along_z * along_z))
        values = jnp.where(lane < fill_ref[plane, tile], values, 0.0)
        start = pl.multiple_of(tile * 16, 16)
        denom_ref[pl.ds(start, 16), :] = jnp.broadcast_to(
            1.0 + jnp.sum(values, axis=1, keepdims=True), (16, 128)
        )
        half = values.astype(BF).astype(F32)
        high = jnp.broadcast_to(near >> 8, (16, slots))
        low = near & 255
        stacked = jnp.concatenate(
            [jnp.where(high == g, half, 0.0).astype(BF) for g in range(groups)], axis=0
        )
        hot = jnp.where(low_ids == low, 1.0, 0.0).astype(BF)
        block = lax.dot_general(
            stacked, hot, (((1,), (1,)), ((), ())), preferred_element_type=F32
        ).astype(BF)
        for g in range(groups):
            rows = block[g * 16 : g * 16 + 16, :]
            if g * 256 < split:
                close[pl.ds(start, 16), g * 256 : g * 256 + 256] = rows
            else:
                out_ref[pl.ds(start, 16), g * 256 - split : g * 256 - split + 256] = rows
        return carry

    lax.fori_loop(0, tiles, one_tile, 0, unroll=4)
    part_ref[...] = jnp.dot(
        close[:, :capacity], t0[...], preferred_element_type=F32
    ) + jnp.dot(close[:, capacity:], t1[...], preferred_element_type=F32)


def spread_weights(near, fill, place, tables):
    planes, tiles, slots = near.shape
    capacity, channels = tables[0].shape
    rows = 2 * capacity
    return pl.pallas_call(
        spread_kernel,
        grid=(planes,),
        in_specs=[
            pl.BlockSpec(memory_space=pltpu.SMEM),
            pl.BlockSpec((1, tiles, slots), lambda z: (z, 0, 0)),
            pl.BlockSpec((1, 3, tiles, slots), lambda z: (z, 0, 0, 0)),
        ]
        + [pl.BlockSpec((capacity, channels), lambda z: (0, 0))] * 2,
        out_specs=[
            pl.BlockSpec((tiles * 16, rows), lambda z: (z, 0)),
            pl.BlockSpec((tiles * 16, channels), lambda z: (z, 0)),
            pl.BlockSpec((tiles * 16, 128), lambda z: (z, 0)),
        ],
        out_shape=[
            jax.ShapeDtypeStruct((planes * tiles * 16, rows), BF),
            jax.ShapeDtypeStruct((planes * tiles * 16, channels), F32),
            jax.ShapeDtypeStruct((planes * tiles * 16, 128), F32),
        ],
        scratch_shapes=[pltpu.VMEM((tiles * 16, rows), BF)],
        compiler_params=pltpu.CompilerParams(vmem_limit_bytes=16 << 20),
    )(fill, near, place, *tables)


def latent_kernel(
    flags_ref, spread_ref, part_ref, denom_ref, t0, t1,
    out_ref, near_ref, far_ref, first_ref, second_ref, total, order,
):
    plane = pl.program_id(0)
    last = pl.num_programs(0) - 1
    core = flags_ref[0]
    odd = flags_ref[2]
    capacity, channels = t0.shape
    cells = spread_ref.shape[0]
    tiles = cells // 16
    summed = part_ref[...]
    for place, table in ((0, t0), (1, t1)):
        summed = summed + jnp.dot(
            spread_ref[:, place * capacity : (place + 1) * capacity],
            table[...],
            preferred_element_type=F32,
        )
    for lanes in range(0, channels, 128):
        part = slice(lanes, lanes + 128)
        total[...] = summed[:, part] / denom_ref[...]
        for u in range(4):
            for v in range(4):
                order[pl.ds(v, tiles, stride=4), :] = total[
                    pl.ds(u * 4 + v, tiles, stride=16), :
                ]
            out_ref[0, u, :, part] = order[...].astype(BF)
    first_ref[0, 0] = out_ref[0, 3 * (1 - odd)]
    second_ref[0, 0] = out_ref[0, 3 * odd]

    @pl.when(plane == (1 - core) * last)
    def _():
        near_ref[...] = out_ref[...]

    @pl.when(plane == core * last)
    def _():
        far_ref[...] = out_ref[...]


def latent_block(flags, spread, part, denom, tables):
    cells = spread.shape[0]
    planes = 4
    per_plane = cells // planes
    capacity, channels = tables[0].shape
    width = per_plane // 4
    whole = pl.BlockSpec((capacity, channels), lambda z: (0, 0))
    plane_spec = pl.BlockSpec((1, 4, width, channels), lambda z: (0, 0, 0, 0))
    row_spec = pl.BlockSpec((1, 1, width, channels), lambda z: (z, 0, 0, 0))
    return pl.pallas_call(
        latent_kernel,
        grid=(planes,),
        in_specs=[
            pl.BlockSpec(memory_space=pltpu.SMEM),
            pl.BlockSpec((per_plane, spread.shape[1]), lambda z: (z, 0)),
            pl.BlockSpec((per_plane, channels), lambda z: (z, 0)),
            pl.BlockSpec((per_plane, 128), lambda z: (z, 0)),
        ]
        + [whole] * 2,
        out_specs=[
            pl.BlockSpec((1, 4, width, channels), lambda z: (z, 0, 0, 0)),
            plane_spec,
            plane_spec,
            row_spec,
            row_spec,
        ],
        out_shape=[
            jax.ShapeDtypeStruct((planes, 4, width, channels), BF),
            jax.ShapeDtypeStruct((1, 4, width, channels), BF),
            jax.ShapeDtypeStruct((1, 4, width, channels), BF),
            jax.ShapeDtypeStruct((planes, 1, width, channels), BF),
            jax.ShapeDtypeStruct((planes, 1, width, channels), BF),
        ],
        scratch_shapes=[
            pltpu.VMEM((per_plane, 128), F32),
            pltpu.VMEM((width, 128), F32),
        ],
        compiler_params=pltpu.CompilerParams(vmem_limit_bytes=20 << 20),
    )(flags, spread, part, denom, *tables)


def with_shifts(taps_ref, start, width, channels, y_ids):
    rows = pl.ds(start, width)
    low = pltpu.roll(taps_ref[rows, 0:channels], 1, 0)
    high = pltpu.roll(taps_ref[rows, 2 * channels :], width - 1, 0)
    return (
        jnp.where(y_ids == 0, 0.0, low)
        + taps_ref[rows, channels : 2 * channels]
        + jnp.where(y_ids == width - 1, 0.0, high)
    )


def times_weight(taps_ref, pieces, weight_ref, positions, channels):
    patch = jnp.concatenate(pieces, axis=1)
    for dy in range(3):
        matrix = jnp.concatenate([weight_ref[p + dy] for p in positions], axis=0)
        taps_ref[:, dy * channels : (dy + 1) * channels] = jnp.dot(
            patch, matrix, preferred_element_type=F32
        )


def inner_kernel(chosen, latent_ref, weight_ref, part_ref, padded, taps):
    planes, rows_x, width, channels = latent_ref.shape
    flat = rows_x * width
    none = jnp.zeros((planes, width, channels), BF)
    padded[:, 0] = none
    padded[:, 1 : rows_x + 1] = latent_ref[...]
    padded[:, rows_x + 1] = none
    y_ids = lax.broadcasted_iota(jnp.int32, (width, channels), 0)
    for place, z in enumerate(chosen):
        reach = [(dz, dx) for dz in range(3) if 0 <= z + dz - 1 < planes for dx in range(3)]
        pieces = [
            padded[z + dz - 1, dx : dx + rows_x].reshape(flat, channels) for dz, dx in reach
        ]
        times_weight(
            taps, pieces, weight_ref, [9 * dz + 3 * dx for dz, dx in reach], channels
        )
        for x in range(rows_x):
            part_ref[place, x] = with_shifts(taps, x * width, width, channels, y_ids)


def inner_conv(chosen, latent, weight):
    planes, rows_x, width, channels = latent.shape
    whole = pl.BlockSpec(memory_space=pltpu.VMEM)
    return pl.pallas_call(
        functools.partial(inner_kernel, chosen),
        in_specs=[whole] * 2,
        out_specs=whole,
        out_shape=jax.ShapeDtypeStruct((len(chosen), rows_x, width, channels), F32),
        scratch_shapes=[
            pltpu.VMEM((planes, rows_x + 2, width, channels), BF),
            pltpu.VMEM((rows_x * width, 3 * channels), F32),
        ],
        compiler_params=pltpu.CompilerParams(vmem_limit_bytes=20 << 20),
        cost_estimate=BRIEF,
    )(latent, weight)


def grad_taps(first, count, core, turned, shifted, keep_ref, give_ref, width):
    planes = turned.shape[0] - 2
    channels = turned.shape[1]
    flat = shifted.shape[0] // planes
    half_size = keep_ref.shape[1]

    def one_tap(index, carry):
        tap = first + index
        dz = tap // 3
        start = pl.multiple_of((tap % 3) * width, width)
        pieces = [turned[z + dz, :, pl.ds(start, flat)] for z in range(planes)]
        sums = jnp.dot(
            jnp.concatenate(pieces, axis=1), shifted[...], preferred_element_type=F32
        )
        for dy in range(3):
            part = sums[:, dy * channels : (dy + 1) * channels]
            both = jnp.concatenate(
                [
                    part[:, :128].reshape(channels // 8, 8, 128),
                    part[:, 128:].reshape(channels // 8, 8, 128),
                ],
                axis=1,
            )
            position = index * 3 + dy
            half = position // half_size
            slot = position - half * half_size
            rounded = both.astype(BF)

            @pl.when(half == core)
            def _():
                keep_ref[:, slot] = rounded

            @pl.when(half != core)
            def _():
                give_ref[:, slot] = rounded

        return carry

    lax.fori_loop(0, count, one_tap, 0)
    if 3 * count < 2 * half_size:
        unused = jnp.zeros((channels // 8, 16, 128), BF)

        @pl.when(core == 1)
        def _():
            keep_ref[:, half_size - 1] = unused

        @pl.when(core == 0)
        def _():
            give_ref[:, half_size - 1] = unused


def outer_kernel(
    flags_ref, middle_ref, edge_ref, latent_ref, near_ref, far_ref, first_ref, second_ref,
    first_end_ref, second_end_ref, weight_ref, bias_ref, cotangent_ref,
    act_ref, turned, shifted, keep_ref, give_ref,
    padded, rims, side_x, side_z,
):
    planes, rows_x, width, channels = latent_ref.shape
    flat = rows_x * width
    core = flags_ref[0]
    has_far = flags_ref[1] > 0
    odd = flags_ref[2]
    has_second = flags_ref[3] > 0
    near_z = (1 - core) * (planes + 1)
    far_z = core * (planes + 1)
    first_x = (1 - odd) * (rows_x + 1)
    second_x = odd * (rows_x + 1)
    none = jnp.zeros((), BF)
    padded[1 : planes + 1, 1 : rows_x + 1] = latent_ref[...]
    padded[near_z, 1 : rows_x + 1] = near_ref[0]
    padded[far_z, 1 : rows_x + 1] = jnp.where(has_far, far_ref[0], none)
    for x, face_ref, end_ref, present in (
        (first_x, first_ref, first_end_ref, True),
        (second_x, second_ref, second_end_ref, has_second),
    ):
        padded[1 : planes + 1, x] = jnp.where(present, face_ref[:, 0], none)
        padded[near_z, x] = jnp.where(present, end_ref[0], none)
        padded[far_z, x] = jnp.where(jnp.logical_and(present, has_far), end_ref[1], none)
    blank = jnp.zeros((width, channels), BF)
    for side in range(2):
        rims[side, 0] = blank
        rims[side, 1 : rows_x + 1] = padded[side * (planes + 1), 1 : rows_x + 1]
        rims[side, rows_x + 1] = blank
    y_ids = lax.broadcasted_iota(jnp.int32, (width, channels), 0)
    root = math.sqrt(2.0 / math.pi)

    def turn(z, carry):
        turned[z] = padded[z].reshape((rows_x + 2) * width, channels).T
        return carry

    lax.fori_loop(0, planes + 2, turn, 0)

    for side in range(2):
        column = side * (rows_x + 1)
        times_weight(
            side_x.at[side],
            [padded[dz : dz + planes, column].reshape(planes * width, channels) for dz in range(3)],
            weight_ref,
            [9 * dz + 6 * side for dz in range(3)],
            channels,
        )
        times_weight(
            side_z.at[side],
            [rims[side, dx : dx + rows_x].reshape(flat, channels) for dx in range(3)],
            weight_ref,
            [18 * side + 3 * dx for dx in range(3)],
            channels,
        )
    for z in range(planes):
        for x in range(rows_x):
            inner_part = edge_ref[int(z > 0), x] if z in (0, planes - 1) else middle_ref[z - 1, x]
            pre = inner_part + bias_ref[...]
            if x in (0, rows_x - 1):
                pre = pre + with_shifts(
                    side_x.at[int(x > 0)], z * width, width, channels, y_ids
                )
            if z in (0, planes - 1):
                pre = pre + with_shifts(
                    side_z.at[int(z > 0)], x * width, width, channels, y_ids
                )
            square = pre * pre
            inner = root * (pre + 0.044715 * (square * pre))
            bent = jnp.tanh(inner)
            gate = 0.5 * (1.0 + bent)
            act_ref[z, x] = (pre * gate).astype(BF)
            slope = gate + 0.5 * pre * (1.0 - bent * bent) * (
                root * (1.0 + 3.0 * 0.044715 * square)
            )
            grad = (cotangent_ref[z, x].astype(F32) * slope).astype(BF).astype(F32)
            rows = pl.ds(z * flat + x * width, width)
            shifted[rows, 0:channels] = jnp.where(
                y_ids == width - 1, 0.0, pltpu.roll(grad, width - 1, 0)
            ).astype(BF)
            shifted[rows, channels : 2 * channels] = grad.astype(BF)
            shifted[rows, 2 * channels :] = jnp.where(
                y_ids == 0, 0.0, pltpu.roll(grad, 1, 0)
            ).astype(BF)
    grad_taps(0, 5, core, turned, shifted, keep_ref, give_ref, width)


def outer_conv(flags, parts, latent, near, far, faces, weight, bias, cotangent):
    planes, rows_x, width, channels = latent.shape
    flat = rows_x * width
    whole = pl.BlockSpec(memory_space=pltpu.VMEM)
    half_terms = jax.ShapeDtypeStruct((channels // 8, 8, 16, 128), BF)
    return pl.pallas_call(
        outer_kernel,
        in_specs=[pl.BlockSpec(memory_space=pltpu.SMEM)] + [whole] * 12,
        out_specs=[whole] * 5,
        out_shape=[
            jax.ShapeDtypeStruct(latent.shape, BF),
            jax.ShapeDtypeStruct((planes + 2, channels, (rows_x + 2) * width), BF),
            jax.ShapeDtypeStruct((planes * flat, 3 * channels), BF),
            half_terms,
            half_terms,
        ],
        scratch_shapes=[
            pltpu.VMEM((planes + 2, rows_x + 2, width, channels), BF),
            pltpu.VMEM((2, rows_x + 2, width, channels), BF),
            pltpu.VMEM((2, planes * width, 3 * channels), F32),
            pltpu.VMEM((2, flat, 3 * channels), F32),
        ],
        compiler_params=pltpu.CompilerParams(vmem_limit_bytes=32 << 20),
    )(flags, *parts, latent, near, far, *faces, weight, bias, cotangent)


def rest_kernel(flags_ref, turned, shifted, keep_ref, give_ref):
    width = turned.shape[2] // 6
    grad_taps(5, 4, flags_ref[0], turned, shifted, keep_ref, give_ref, width)


def rest_terms(flags, turned, shifted):
    channels = turned.shape[1]
    whole = pl.BlockSpec(memory_space=pltpu.VMEM)
    half_terms = jax.ShapeDtypeStruct((channels // 8, 6, 16, 128), BF)
    return pl.pallas_call(
        rest_kernel,
        in_specs=[pl.BlockSpec(memory_space=pltpu.SMEM)] + [whole] * 2,
        out_specs=[whole] * 2,
        out_shape=[half_terms] * 2,
        compiler_params=pltpu.CompilerParams(vmem_limit_bytes=20 << 20),
    )(flags, turned, shifted)


def pair_sum(keep, give, swap):
    paired = keep.astype(F32) + lax.ppermute(give, "space", swap).astype(F32)
    return paired.astype(BF).reshape((2, 4, 4) + keep.shape[1:])


def sum_over(block, step, count, dim):
    chans = lax.axis_size("chan")
    index = lax.rem(lax.axis_index("chan") // step, count)
    total = lax.dynamic_index_in_dim(block, index, dim, keepdims=False).astype(F32)
    for offset in range(1, count):
        part = lax.dynamic_index_in_dim(block, index ^ offset, dim, keepdims=False)
        total = total + lax.ppermute(
            part, "chan", [(i, i ^ (offset * step)) for i in range(chans)]
        ).astype(F32)
    return total


def chan_pieces(array, step, count):
    chans = lax.axis_size("chan")
    return [array] + [
        lax.ppermute(array, "chan", [(i, i ^ (offset * step)) for i in range(chans)])
        for offset in range(1, count)
    ]


def in_place(index, pieces):
    result = jnp.zeros((len(pieces),) + pieces[0].shape, BF)
    for offset, piece in enumerate(pieces):
        result = lax.dynamic_update_index_in_dim(result, piece, index ^ offset, 0)
    return result


def in_order(core, own, other):
    low = jnp.where(core == 0, own, other)
    high = jnp.where(core == 0, other, own)
    return low, high


def on_device(
    point_feats,
    send_slots,
    send_counts,
    neighbors,
    tile_fill,
    offsets,
    weight,
    conv_bias,
    cotangent,
):
    spaces = lax.axis_size("space")
    chans = lax.axis_size("chan")
    planes, rows_x, width_y, channels = cotangent.shape
    row_count = weight.shape[0]
    space = lax.axis_index("space")
    chan = lax.axis_index("chan")
    core = lax.rem(space, 2)
    swap = [(i, i ^ 1) for i in range(spaces)]
    far = [(i, i ^ 2) for i in range(spaces)]
    cross = [(i, i ^ 3) for i in range(spaces)]
    first_pairs = [(i, i ^ 1) for i in range(chans)]
    second_pairs = [(i, (i - 1 + 2 * (i % 2)) % chans) for i in range(chans)]
    flags = jnp.stack(
        [
            core,
            jnp.logical_or(space == 1, space == 2).astype(jnp.int32),
            lax.rem(chan, 2),
            jnp.logical_and(chan > 0, chan < chans - 1).astype(jnp.int32),
        ]
    )

    taps = jnp.pad(weight.transpose(1, 0, 2), ((0, 1), (0, 0), (0, 0)))
    gathered = lax.dynamic_slice_in_dim(taps, core * 14, 14, 0)
    gathered = in_place(chan // 16, chan_pieces(gathered, 16, 2))

    slots, counts = send_slots[0, 0], send_counts[0, 0]
    capacity = slots.shape[1]
    slots = slots.reshape(spaces, capacity // 128, 128)
    owners = space ^ jnp.arange(spaces, dtype=jnp.int32)
    scalars = jnp.concatenate([owners.reshape(2, 2), counts[owners].reshape(2, 2)], axis=1)
    to_far, to_cross = gather_listed(point_feats, slots, scalars[1])
    to_far, to_cross, gathered = lax.optimization_barrier((to_far, to_cross, gathered))
    from_far = lax.ppermute(to_far, "space", far)
    from_cross = lax.ppermute(to_cross, "space", cross)
    gathered = jnp.broadcast_to(gathered[None], (16,) + gathered.shape)
    gathered = lax.all_to_all(
        gathered,
        "chan",
        split_axis=0,
        concat_axis=0,
        axis_index_groups=[[16 * y + i for i in range(16)] for y in range(chans // 16)],
        tiled=True,
    )
    held_scalars, _ = lax.optimization_barrier((scalars[0], to_far))
    to_self, to_other = gather_listed(point_feats, slots, held_scalars)
    from_other = lax.ppermute(to_other, "space", swap)

    near, _ = lax.optimization_barrier((neighbors[:, 0], to_self))
    spread, close_part, denom = spread_weights(
        near ^ (space * capacity),
        tile_fill[:, 0],
        offsets[:, 0].transpose(0, 2, 1, 3),
        (to_self, from_other),
    )

    latent, near_plane, far_plane, first_row, second_row = latent_block(
        flags, spread, close_part, denom, (from_far, from_cross)
    )

    far_rim = lax.ppermute(far_plane, "space", cross)
    near_rim = lax.ppermute(near_plane, "space", swap)
    gathered, _ = lax.optimization_barrier((gathered, near_plane))
    gathered = jnp.stack(in_order(core, gathered, lax.ppermute(gathered, "space", swap)))
    full_weight = gathered.transpose(0, 3, 2, 1, 4, 5).reshape(28, channels, channels)
    faces = [
        lax.ppermute(first_row, "chan", first_pairs),
        lax.ppermute(second_row, "chan", second_pairs),
    ]
    middle = inner_conv((1, 2), latent, full_weight)
    far_rim, near_rim, middle = lax.optimization_barrier((far_rim, near_rim, middle))
    odd = lax.rem(chan, 2)
    corners = []
    for side, pairs in ((1 - odd, first_pairs), (odd, second_pairs)):
        ends = [
            lax.dynamic_index_in_dim(rim, (rows_x - 1) * side, 1, keepdims=False)
            for rim in (near_rim, far_rim)
        ]
        ends = jnp.concatenate(ends, axis=0)
        corners.append(lax.ppermute(ends, "chan", pairs))
        held_latent = lax.optimization_barrier((latent, ends))[0]
    edge = inner_conv((0, 3), held_latent, full_weight)

    activated, turned, shifted, keep, give = outer_conv(
        flags, (middle, edge), latent, near_rim, far_rim, (*faces, *corners),
        full_weight, conv_bias.astype(F32)[None], cotangent,
    )
    early = pair_sum(keep, give, swap)
    held_flags, early = lax.optimization_barrier((flags, early))
    late = pair_sum(*rest_terms(held_flags, turned, shifted), swap)
    early = sum_over(early, 1, 4, 2).astype(BF)
    late = sum_over(late, 4, 4, 1).astype(BF)
    early = sum_over(early, 4, 4, 1)
    late = sum_over(late, 1, 4, 1)
    summed = sum_over(jnp.concatenate([early, late], axis=1), 16, 2, 0)
    own_sum = summed + lax.ppermute(summed, "space", far)
    low_sum, high_sum = in_order(core, own_sum, lax.ppermute(own_sum, "space", swap))
    total = jnp.concatenate([low_sum[:8], high_sum[:7], low_sum[8:], high_sum[8:]], axis=0)
    total = total.reshape(27, 2, row_count, channels // 2).transpose(2, 0, 1, 3)
    scaling = 1.0 / math.sqrt(planes * spaces * rows_x * chans * width_y)
    return (activated, total.reshape(row_count, 27, channels) * scaling)


def solution(mesh):
    return jax.shard_map(
        on_device,
        mesh=mesh,
        in_specs=(
            P(("space", "chan"), None),
            P("space", "chan", None, None),
            P("space", "chan", None),
            P("space", "chan", None, None),
            P("space", "chan", None),
            P("space", "chan", None, None, None),
            P("chan", None, None),
            P(),
            P("space", "chan", None, None),
        ),
        out_specs=(P("space", "chan", None, None), P("chan", None, None)),
        check_vma=False,
    )
```

```python
import functools
import math

import jax
import jax.numpy as jnp
from jax import lax
from jax.experimental import pallas as pl
from jax.experimental.pallas import tpu as pltpu
from jax.sharding import PartitionSpec as P

BF = jnp.bfloat16
F32 = jnp.float32
BRIEF = pl.CostEstimate(flops=1, bytes_accessed=1, transcendentals=0)


def send_kernel(scalars_ref, slots_ref, feats_ref, *out_refs):
    points = feats_ref.shape[0]
    point_ids = lax.broadcasted_iota(jnp.int32, (128, points), 1)
    for place, out_ref in enumerate(out_refs):
        owner = scalars_ref[place]
        columns = slots_ref[owner].T
        for half in range(2):
            hot = [
                jnp.where(point_ids == columns[:, r : r + 1], 1.0, 0.0).astype(BF)
                for r in range(half * 4, half * 4 + 4)
            ]
            rows = jnp.dot(
                jnp.concatenate(hot, axis=0), feats_ref[...], preferred_element_type=F32
            )
            out_ref[half * 512 : half * 512 + 512, :] = rows.astype(BF)


def gather_listed(feats, slots, scalars):
    capacity = slots.shape[1] * slots.shape[2]
    channels = feats.shape[1]
    whole = pl.BlockSpec(memory_space=pltpu.VMEM)
    return pl.pallas_call(
        send_kernel,
        in_specs=[pl.BlockSpec(memory_space=pltpu.SMEM), whole, whole],
        out_specs=[whole] * 2,
        out_shape=[jax.ShapeDtypeStruct((capacity, channels), BF)] * 2,
        compiler_params=pltpu.CompilerParams(vmem_limit_bytes=16 << 20),
        cost_estimate=BRIEF,
    )(scalars, slots, feats)


def spread_kernel(fill_ref, near_ref, place_ref, t0, t1, out_ref, part_ref, denom_ref, close):
    plane = pl.program_id(0)
    tiles = near_ref.shape[1]
    slots = near_ref.shape[2]
    groups = (out_ref.shape[1] + close.shape[1]) // 256
    split = close.shape[1]
    capacity = t0.shape[0]
    cell = lax.broadcasted_iota(jnp.int32, (16, slots), 0)
    centre_x = (cell // 4).astype(F32) - 1.5
    centre_y = (cell % 4).astype(F32) - 1.5
    lane = lax.broadcasted_iota(jnp.int32, (16, slots), 1)
    low_ids = lax.broadcasted_iota(jnp.int32, (256, slots), 0)

    def one_tile(tile, carry):
        near = near_ref[0, pl.ds(tile, 1), :]
        along_x = place_ref[0, 0, pl.ds(tile, 1), :] - centre_x
        along_y = place_ref[0, 1, pl.ds(tile, 1), :] - centre_y
        along_z = place_ref[0, 2, pl.ds(tile, 1), :]
        values = jnp.exp(-0.5 * (along_x * along_x + along_y * along_y + along_z * along_z))
        values = jnp.where(lane < fill_ref[plane, tile], values, 0.0)
        start = pl.multiple_of(tile * 16, 16)
        denom_ref[pl.ds(start, 16), :] = jnp.broadcast_to(
            1.0 + jnp.sum(values, axis=1, keepdims=True), (16, 128)
        )
        half = values.astype(BF).astype(F32)
        high = jnp.broadcast_to(near >> 8, (16, slots))
        low = near & 255
        stacked = jnp.concatenate(
            [jnp.where(high == g, half, 0.0).astype(BF) for g in range(groups)], axis=0
        )
        hot = jnp.where(low_ids == low, 1.0, 0.0).astype(BF)
        block = lax.dot_general(
            stacked, hot, (((1,), (1,)), ((), ())), preferred_element_type=F32
        ).astype(BF)
        for g in range(groups):
            rows = block[g * 16 : g * 16 + 16, :]
            if g * 256 < split:
                close[pl.ds(start, 16), g * 256 : g * 256 + 256] = rows
            else:
                out_ref[pl.ds(start, 16), g * 256 - split : g * 256 - split + 256] = rows
        return carry

    lax.fori_loop(0, tiles, one_tile, 0, unroll=4)
    part_ref[...] = jnp.dot(
        close[:, :capacity], t0[...], preferred_element_type=F32
    ) + jnp.dot(close[:, capacity:], t1[...], preferred_element_type=F32)


def spread_weights(near, fill, place, tables):
    planes, tiles, slots = near.shape
    capacity, channels = tables[0].shape
    rows = 2 * capacity
    return pl.pallas_call(
        spread_kernel,
        grid=(planes,),
        in_specs=[
            pl.BlockSpec(memory_space=pltpu.SMEM),
            pl.BlockSpec((1, tiles, slots), lambda z: (z, 0, 0)),
            pl.BlockSpec((1, 3, tiles, slots), lambda z: (z, 0, 0, 0)),
        ]
        + [pl.BlockSpec((capacity, channels), lambda z: (0, 0))] * 2,
        out_specs=[
            pl.BlockSpec((tiles * 16, rows), lambda z: (z, 0)),
            pl.BlockSpec((tiles * 16, channels), lambda z: (z, 0)),
            pl.BlockSpec((tiles * 16, 128), lambda z: (z, 0)),
        ],
        out_shape=[
            jax.ShapeDtypeStruct((planes * tiles * 16, rows), BF),
            jax.ShapeDtypeStruct((planes * tiles * 16, channels), F32),
            jax.ShapeDtypeStruct((planes * tiles * 16, 128), F32),
        ],
        scratch_shapes=[pltpu.VMEM((tiles * 16, rows), BF)],
        compiler_params=pltpu.CompilerParams(vmem_limit_bytes=16 << 20),
    )(fill, near, place, *tables)


def latent_kernel(
    flags_ref, spread_ref, part_ref, denom_ref, t0, t1,
    out_ref, near_ref, far_ref, first_ref, second_ref, total, order,
):
    plane = pl.program_id(0)
    last = pl.num_programs(0) - 1
    core = flags_ref[0]
    odd = flags_ref[2]
    capacity, channels = t0.shape
    cells = spread_ref.shape[0]
    tiles = cells // 16
    summed = part_ref[...]
    for place, table in ((0, t0), (1, t1)):
        summed = summed + jnp.dot(
            spread_ref[:, place * capacity : (place + 1) * capacity],
            table[...],
            preferred_element_type=F32,
        )
    for lanes in range(0, channels, 128):
        part = slice(lanes, lanes + 128)
        total[...] = summed[:, part] / denom_ref[...]
        for u in range(4):
            for v in range(4):
                order[pl.ds(v, tiles, stride=4), :] = total[
                    pl.ds(u * 4 + v, tiles, stride=16), :
                ]
            out_ref[0, u, :, part] = order[...].astype(BF)
    first_ref[0, 0] = out_ref[0, 3 * (1 - odd)]
    second_ref[0, 0] = out_ref[0, 3 * odd]

    @pl.when(plane == (1 - core) * last)
    def _():
        near_ref[...] = out_ref[...]

    @pl.when(plane == core * last)
    def _():
        far_ref[...] = out_ref[...]


def latent_block(flags, spread, part, denom, tables):
    cells = spread.shape[0]
    planes = 4
    per_plane = cells // planes
    capacity, channels = tables[0].shape
    width = per_plane // 4
    whole = pl.BlockSpec((capacity, channels), lambda z: (0, 0))
    plane_spec = pl.BlockSpec((1, 4, width, channels), lambda z: (0, 0, 0, 0))
    row_spec = pl.BlockSpec((1, 1, width, channels), lambda z: (z, 0, 0, 0))
    return pl.pallas_call(
        latent_kernel,
        grid=(planes,),
        in_specs=[
            pl.BlockSpec(memory_space=pltpu.SMEM),
            pl.BlockSpec((per_plane, spread.shape[1]), lambda z: (z, 0)),
            pl.BlockSpec((per_plane, channels), lambda z: (z, 0)),
            pl.BlockSpec((per_plane, 128), lambda z: (z, 0)),
        ]
        + [whole] * 2,
        out_specs=[
            pl.BlockSpec((1, 4, width, channels), lambda z: (z, 0, 0, 0)),
            plane_spec,
            plane_spec,
            row_spec,
            row_spec,
        ],
        out_shape=[
            jax.ShapeDtypeStruct((planes, 4, width, channels), BF),
            jax.ShapeDtypeStruct((1, 4, width, channels), BF),
            jax.ShapeDtypeStruct((1, 4, width, channels), BF),
            jax.ShapeDtypeStruct((planes, 1, width, channels), BF),
            jax.ShapeDtypeStruct((planes, 1, width, channels), BF),
        ],
        scratch_shapes=[
            pltpu.VMEM((per_plane, 128), F32),
            pltpu.VMEM((width, 128), F32),
        ],
        compiler_params=pltpu.CompilerParams(vmem_limit_bytes=20 << 20),
    )(flags, spread, part, denom, *tables)


def with_shifts(taps_ref, start, width, channels, y_ids):
    rows = pl.ds(start, width)
    low = pltpu.roll(taps_ref[rows, 0:channels], 1, 0)
    high = pltpu.roll(taps_ref[rows, 2 * channels :], width - 1, 0)
    return (
        jnp.where(y_ids == 0, 0.0, low)
        + taps_ref[rows, channels : 2 * channels]
        + jnp.where(y_ids == width - 1, 0.0, high)
    )


def times_weight(taps_ref, pieces, weight_ref, positions, channels):
    patch = jnp.concatenate(pieces, axis=1)
    for dy in range(3):
        matrix = jnp.concatenate([weight_ref[p + dy] for p in positions], axis=0)
        taps_ref[:, dy * channels : (dy + 1) * channels] = jnp.dot(
            patch, matrix, preferred_element_type=F32
        )


def inner_kernel(chosen, latent_ref, weight_ref, part_ref, padded, taps):
    planes, rows_x, width, channels = latent_ref.shape
    flat = rows_x * width
    none = jnp.zeros((planes, width, channels), BF)
    padded[:, 0] = none
    padded[:, 1 : rows_x + 1] = latent_ref[...]
    padded[:, rows_x + 1] = none
    y_ids = lax.broadcasted_iota(jnp.int32, (width, channels), 0)
    for place, z in enumerate(chosen):
        reach = [(dz, dx) for dz in range(3) if 0 <= z + dz - 1 < planes for dx in range(3)]
        pieces = [
            padded[z + dz - 1, dx : dx + rows_x].reshape(flat, channels) for dz, dx in reach
        ]
        times_weight(
            taps, pieces, weight_ref, [9 * dz + 3 * dx for dz, dx in reach], channels
        )
        for x in range(rows_x):
            part_ref[place, x] = with_shifts(taps, x * width, width, channels, y_ids)


def inner_conv(chosen, latent, weight):
    planes, rows_x, width, channels = latent.shape
    whole = pl.BlockSpec(memory_space=pltpu.VMEM)
    return pl.pallas_call(
        functools.partial(inner_kernel, chosen),
        in_specs=[whole] * 2,
        out_specs=whole,
        out_shape=jax.ShapeDtypeStruct((len(chosen), rows_x, width, channels), F32),
        scratch_shapes=[
            pltpu.VMEM((planes, rows_x + 2, width, channels), BF),
            pltpu.VMEM((rows_x * width, 3 * channels), F32),
        ],
        compiler_params=pltpu.CompilerParams(vmem_limit_bytes=20 << 20),
        cost_estimate=BRIEF,
    )(latent, weight)


def grad_taps(first, count, core, turned, shifted, keep_ref, give_ref, width):
    planes = turned.shape[0] - 2
    channels = turned.shape[1]
    flat = shifted.shape[0] // planes
    half_size = keep_ref.shape[1]

    def one_tap(index, carry):
        tap = first + index
        dz = tap // 3
        start = pl.multiple_of((tap % 3) * width, width)
        pieces = [turned[z + dz, :, pl.ds(start, flat)] for z in range(planes)]
        sums = jnp.dot(
            jnp.concatenate(pieces, axis=1), shifted[...], preferred_element_type=F32
        )
        for dy in range(3):
            part = sums[:, dy * channels : (dy + 1) * channels]
            both = jnp.concatenate(
                [
                    part[:, :128].reshape(channels // 8, 8, 128),
                    part[:, 128:].reshape(channels // 8, 8, 128),
                ],
                axis=1,
            )
            position = index * 3 + dy
            half = position // half_size
            slot = position - half * half_size
            rounded = both.astype(BF)

            @pl.when(half == core)
            def _():
                keep_ref[:, slot] = rounded

            @pl.when(half != core)
            def _():
                give_ref[:, slot] = rounded

        return carry

    lax.fori_loop(0, count, one_tap, 0)
    if 3 * count < 2 * half_size:
        unused = jnp.zeros((channels // 8, 16, 128), BF)

        @pl.when(core == 1)
        def _():
            keep_ref[:, half_size - 1] = unused

        @pl.when(core == 0)
        def _():
            give_ref[:, half_size - 1] = unused


def outer_kernel(
    flags_ref, middle_ref, edge_ref, latent_ref, near_ref, far_ref, first_ref, second_ref,
    first_end_ref, second_end_ref, weight_ref, bias_ref, cotangent_ref,
    act_ref, turned, shifted, keep_ref, give_ref,
    padded, rims, side_x, side_z,
):
    planes, rows_x, width, channels = latent_ref.shape
    flat = rows_x * width
    core = flags_ref[0]
    has_far = flags_ref[1] > 0
    odd = flags_ref[2]
    has_second = flags_ref[3] > 0
    near_z = (1 - core) * (planes + 1)
    far_z = core * (planes + 1)
    first_x = (1 - odd) * (rows_x + 1)
    second_x = odd * (rows_x + 1)
    none = jnp.zeros((), BF)
    padded[1 : planes + 1, 1 : rows_x + 1] = latent_ref[...]
    padded[near_z, 1 : rows_x + 1] = near_ref[0]
    padded[far_z, 1 : rows_x + 1] = jnp.where(has_far, far_ref[0], none)
    for x, face_ref, end_ref, present in (
        (first_x, first_ref, first_end_ref, True),
        (second_x, second_ref, second_end_ref, has_second),
    ):
        padded[1 : planes + 1, x] = jnp.where(present, face_ref[:, 0], none)
        padded[near_z, x] = jnp.where(present, end_ref[0], none)
        padded[far_z, x] = jnp.where(jnp.logical_and(present, has_far), end_ref[1], none)
    blank = jnp.zeros((width, channels), BF)
    for side in range(2):
        rims[side, 0] = blank
        rims[side, 1 : rows_x + 1] = padded[side * (planes + 1), 1 : rows_x + 1]
        rims[side, rows_x + 1] = blank
    y_ids = lax.broadcasted_iota(jnp.int32, (width, channels), 0)
    root = math.sqrt(2.0 / math.pi)

    def turn(z, carry):
        turned[z] = padded[z].reshape((rows_x + 2) * width, channels).T
        return carry

    lax.fori_loop(0, planes + 2, turn, 0)

    for side in range(2):
        column = side * (rows_x + 1)
        times_weight(
            side_x.at[side],
            [padded[dz : dz + planes, column].reshape(planes * width, channels) for dz in range(3)],
            weight_ref,
            [9 * dz + 6 * side for dz in range(3)],
            channels,
        )
        times_weight(
            side_z.at[side],
            [rims[side, dx : dx + rows_x].reshape(flat, channels) for dx in range(3)],
            weight_ref,
            [18 * side + 3 * dx for dx in range(3)],
            channels,
        )
    for z in range(planes):
        for x in range(rows_x):
            inner_part = middle_ref[0, x] if z == 1 else edge_ref[max(z - 1, 0), x]
            pre = inner_part + bias_ref[...]
            if x in (0, rows_x - 1):
                pre = pre + with_shifts(
                    side_x.at[int(x > 0)], z * width, width, channels, y_ids
                )
            if z in (0, planes - 1):
                pre = pre + with_shifts(
                    side_z.at[int(z > 0)], x * width, width, channels, y_ids
                )
            square = pre * pre
            inner = root * (pre + 0.044715 * (square * pre))
            bent = jnp.tanh(inner)
            gate = 0.5 * (1.0 + bent)
            act_ref[z, x] = (pre * gate).astype(BF)
            slope = gate + 0.5 * pre * (1.0 - bent * bent) * (
                root * (1.0 + 3.0 * 0.044715 * square)
            )
            grad = (cotangent_ref[z, x].astype(F32) * slope).astype(BF).astype(F32)
            rows = pl.ds(z * flat + x * width, width)
            shifted[rows, 0:channels] = jnp.where(
                y_ids == width - 1, 0.0, pltpu.roll(grad, width - 1, 0)
            ).astype(BF)
            shifted[rows, channels : 2 * channels] = grad.astype(BF)
            shifted[rows, 2 * channels :] = jnp.where(
                y_ids == 0, 0.0, pltpu.roll(grad, 1, 0)
            ).astype(BF)
    grad_taps(0, 5, core, turned, shifted, keep_ref, give_ref, width)


def outer_conv(flags, parts, latent, near, far, faces, weight, bias, cotangent):
    planes, rows_x, width, channels = latent.shape
    flat = rows_x * width
    whole = pl.BlockSpec(memory_space=pltpu.VMEM)
    half_terms = jax.ShapeDtypeStruct((channels // 8, 8, 16, 128), BF)
    return pl.pallas_call(
        outer_kernel,
        in_specs=[pl.BlockSpec(memory_space=pltpu.SMEM)] + [whole] * 12,
        out_specs=[whole] * 5,
        out_shape=[
            jax.ShapeDtypeStruct(latent.shape, BF),
            jax.ShapeDtypeStruct((planes + 2, channels, (rows_x + 2) * width), BF),
            jax.ShapeDtypeStruct((planes * flat, 3 * channels), BF),
            half_terms,
            half_terms,
        ],
        scratch_shapes=[
            pltpu.VMEM((planes + 2, rows_x + 2, width, channels), BF),
            pltpu.VMEM((2, rows_x + 2, width, channels), BF),
            pltpu.VMEM((2, planes * width, 3 * channels), F32),
            pltpu.VMEM((2, flat, 3 * channels), F32),
        ],
        compiler_params=pltpu.CompilerParams(vmem_limit_bytes=32 << 20),
    )(flags, *parts, latent, near, far, *faces, weight, bias, cotangent)


def rest_kernel(flags_ref, turned, shifted, keep_ref, give_ref):
    width = turned.shape[2] // 6
    grad_taps(5, 4, flags_ref[0], turned, shifted, keep_ref, give_ref, width)


def rest_terms(flags, turned, shifted):
    channels = turned.shape[1]
    whole = pl.BlockSpec(memory_space=pltpu.VMEM)
    half_terms = jax.ShapeDtypeStruct((channels // 8, 6, 16, 128), BF)
    return pl.pallas_call(
        rest_kernel,
        in_specs=[pl.BlockSpec(memory_space=pltpu.SMEM)] + [whole] * 2,
        out_specs=[whole] * 2,
        out_shape=[half_terms] * 2,
        compiler_params=pltpu.CompilerParams(vmem_limit_bytes=20 << 20),
    )(flags, turned, shifted)


def pair_sum(keep, give, swap):
    paired = keep.astype(F32) + lax.ppermute(give, "space", swap).astype(F32)
    return paired.astype(BF).reshape((2, 4, 4) + keep.shape[1:])


def sum_over(block, step, count, dim):
    chans = lax.axis_size("chan")
    index = lax.rem(lax.axis_index("chan") // step, count)
    total = lax.dynamic_index_in_dim(block, index, dim, keepdims=False).astype(F32)
    for offset in range(1, count):
        part = lax.dynamic_index_in_dim(block, index ^ offset, dim, keepdims=False)
        total = total + lax.ppermute(
            part, "chan", [(i, i ^ (offset * step)) for i in range(chans)]
        ).astype(F32)
    return total


def chan_pieces(array, step, count):
    chans = lax.axis_size("chan")
    return [array] + [
        lax.ppermute(array, "chan", [(i, i ^ (offset * step)) for i in range(chans)])
        for offset in range(1, count)
    ]


def in_place(index, pieces):
    result = jnp.zeros((len(pieces),) + pieces[0].shape, BF)
    for offset, piece in enumerate(pieces):
        result = lax.dynamic_update_index_in_dim(result, piece, index ^ offset, 0)
    return result


def in_order(core, own, other):
    low = jnp.where(core == 0, own, other)
    high = jnp.where(core == 0, other, own)
    return low, high


def on_device(
    point_feats,
    send_slots,
    send_counts,
    neighbors,
    tile_fill,
    offsets,
    weight,
    conv_bias,
    cotangent,
):
    spaces = lax.axis_size("space")
    chans = lax.axis_size("chan")
    planes, rows_x, width_y, channels = cotangent.shape
    row_count = weight.shape[0]
    space = lax.axis_index("space")
    chan = lax.axis_index("chan")
    core = lax.rem(space, 2)
    swap = [(i, i ^ 1) for i in range(spaces)]
    far = [(i, i ^ 2) for i in range(spaces)]
    cross = [(i, i ^ 3) for i in range(spaces)]
    first_pairs = [(i, i ^ 1) for i in range(chans)]
    second_pairs = [(i, (i - 1 + 2 * (i % 2)) % chans) for i in range(chans)]
    flags = jnp.stack(
        [
            core,
            jnp.logical_or(space == 1, space == 2).astype(jnp.int32),
            lax.rem(chan, 2),
            jnp.logical_and(chan > 0, chan < chans - 1).astype(jnp.int32),
        ]
    )

    taps = jnp.pad(weight.transpose(1, 0, 2), ((0, 1), (0, 0), (0, 0)))
    gathered = lax.dynamic_slice_in_dim(taps, core * 14, 14, 0)
    gathered = in_place(chan // 16, chan_pieces(gathered, 16, 2))

    slots, counts = send_slots[0, 0], send_counts[0, 0]
    capacity = slots.shape[1]
    listed = jnp.arange(capacity, dtype=jnp.int32) < counts[:, None]
    slots = jnp.where(listed, slots, -1).reshape(spaces, capacity // 128, 128)
    scalars = (space ^ jnp.arange(spaces, dtype=jnp.int32)).reshape(2, 2)
    to_far, to_cross = gather_listed(point_feats, slots, scalars[1])
    to_far, to_cross, gathered = lax.optimization_barrier((to_far, to_cross, gathered))
    from_far = lax.ppermute(to_far, "space", far)
    from_cross = lax.ppermute(to_cross, "space", cross)
    gathered = jnp.broadcast_to(gathered[None], (16,) + gathered.shape)
    gathered = lax.all_to_all(
        gathered,
        "chan",
        split_axis=0,
        concat_axis=0,
        axis_index_groups=[[16 * y + i for i in range(16)] for y in range(chans // 16)],
        tiled=True,
    )
    held_scalars, _ = lax.optimization_barrier((scalars[0], to_far))
    to_self, to_other = gather_listed(point_feats, slots, held_scalars)
    from_other = lax.ppermute(to_other, "space", swap)

    near, _ = lax.optimization_barrier((neighbors[:, 0], to_self))
    spread, close_part, denom = spread_weights(
        near ^ (space * capacity),
        tile_fill[:, 0],
        offsets[:, 0].transpose(0, 2, 1, 3),
        (to_self, from_other),
    )

    latent, near_plane, far_plane, first_row, second_row = latent_block(
        flags, spread, close_part, denom, (from_far, from_cross)
    )

    far_rim = lax.ppermute(far_plane, "space", cross)
    near_rim = lax.ppermute(near_plane, "space", swap)
    gathered, _ = lax.optimization_barrier((gathered, near_plane))
    gathered = jnp.stack(in_order(core, gathered, lax.ppermute(gathered, "space", swap)))
    full_weight = gathered.transpose(0, 3, 2, 1, 4, 5).reshape(28, channels, channels)
    faces = [
        lax.ppermute(first_row, "chan", first_pairs),
        lax.ppermute(second_row, "chan", second_pairs),
    ]
    middle = inner_conv((1,), latent, full_weight)
    far_rim, near_rim, middle = lax.optimization_barrier((far_rim, near_rim, middle))
    odd = lax.rem(chan, 2)
    corners = []
    for side, pairs in ((1 - odd, first_pairs), (odd, second_pairs)):
        ends = [
            lax.dynamic_index_in_dim(rim, (rows_x - 1) * side, 1, keepdims=False)
            for rim in (near_rim, far_rim)
        ]
        ends = jnp.concatenate(ends, axis=0)
        corners.append(lax.ppermute(ends, "chan", pairs))
        held_latent = lax.optimization_barrier((latent, ends))[0]
    edge = inner_conv((0, 2, 3), held_latent, full_weight)

    activated, turned, shifted, keep, give = outer_conv(
        flags, (middle, edge), latent, near_rim, far_rim, (*faces, *corners),
        full_weight, conv_bias.astype(F32)[None], cotangent,
    )
    early = pair_sum(keep, give, swap)
    held_flags, early = lax.optimization_barrier((flags, early))
    late = pair_sum(*rest_terms(held_flags, turned, shifted), swap)
    early = sum_over(early, 1, 4, 2).astype(BF)
    late = sum_over(late, 4, 4, 1).astype(BF)
    early = sum_over(early, 4, 4, 1)
    late = sum_over(late, 1, 4, 1)
    both = jnp.concatenate([early, late], axis=1)
    y_low = chan // 16
    kept = lax.dynamic_index_in_dim(both, y_low, 0, keepdims=False)
    passed = lax.dynamic_index_in_dim(both, 1 - y_low, 0, keepdims=False).astype(BF)
    over = [(i, i ^ 16) for i in range(chans)]
    far_over = [(i, i ^ (2 * chans) ^ 16) for i in range(spaces * chans)]
    own_sum = (
        kept
        + lax.ppermute(passed, "chan", over).astype(F32)
        + lax.ppermute(passed, ("space", "chan"), far_over).astype(F32)
        + lax.ppermute(kept.astype(BF), "space", far).astype(F32)
    )
    low_sum, high_sum = in_order(core, own_sum, lax.ppermute(own_sum, "space", swap))
    total = jnp.concatenate([low_sum[:8], high_sum[:7], low_sum[8:], high_sum[8:]], axis=0)
    total = total.reshape(27, 2, row_count, channels // 2).transpose(2, 0, 1, 3)
    scaling = 1.0 / math.sqrt(planes * spaces * rows_x * chans * width_y)
    return (activated, total.reshape(row_count, 27, channels) * scaling)


def solution(mesh):
    return jax.shard_map(
        on_device,
        mesh=mesh,
        in_specs=(
            P(("space", "chan"), None),
            P("space", "chan", None, None),
            P("space", "chan", None),
            P("space", "chan", None, None),
            P("space", "chan", None),
            P("space", "chan", None, None, None),
            P("chan", None, None),
            P(),
            P("space", "chan", None, None),
        ),
        out_specs=(P("space", "chan", None, None), P("chan", None, None)),
        check_vma=False,
    )
```

```python
import functools
import math

import jax
import jax.numpy as jnp
from jax import lax
from jax.experimental import pallas as pl
from jax.experimental.pallas import tpu as pltpu
from jax.sharding import PartitionSpec as P

BF = jnp.bfloat16
F32 = jnp.float32
BRIEF = pl.CostEstimate(flops=1, bytes_accessed=1, transcendentals=0)


def listed_rows(slots, feats_ref, out_ref):
    points = feats_ref.shape[0]
    point_ids = lax.broadcasted_iota(jnp.int32, (128, points), 1)
    columns = slots.T
    for half in range(2):
        hot = [
            jnp.where(point_ids == columns[:, r : r + 1], 1.0, 0.0).astype(BF)
            for r in range(half * 4, half * 4 + 4)
        ]
        rows = jnp.dot(
            jnp.concatenate(hot, axis=0), feats_ref[...], preferred_element_type=F32
        )
        out_ref[half * 512 : half * 512 + 512, :] = rows.astype(BF)


def send_kernel(owners_ref, slots_ref, feats_ref, *out_refs):
    for place, out_ref in enumerate(out_refs):
        listed_rows(slots_ref[owners_ref[place + 1]], feats_ref, out_ref)


def gather_listed(feats, slots, owners):
    count, rows, lanes = slots.shape
    whole = pl.BlockSpec(memory_space=pltpu.VMEM)
    return pl.pallas_call(
        send_kernel,
        in_specs=[pl.BlockSpec(memory_space=pltpu.SMEM), whole, whole],
        out_specs=[whole] * (count - 1),
        out_shape=[jax.ShapeDtypeStruct((rows * lanes, feats.shape[1]), BF)] * (count - 1),
        compiler_params=pltpu.CompilerParams(vmem_limit_bytes=16 << 20),
        cost_estimate=BRIEF,
    )(owners, slots, feats)


def spread_kernel(
    fill_ref, owners_ref, near_ref, place_ref, slots_ref, feats_ref, t1,
    out_ref, part_ref, denom_ref, close, t0,
):
    plane = pl.program_id(0)
    tiles = near_ref.shape[1]
    slots = near_ref.shape[2]
    groups = (out_ref.shape[1] + close.shape[1]) // 256
    split = close.shape[1]
    capacity = t0.shape[0]

    @pl.when(plane == 0)
    def _():
        listed_rows(slots_ref[owners_ref[0]], feats_ref, t0)

    cell = lax.broadcasted_iota(jnp.int32, (16, slots), 0)
    centre_x = (cell // 4).astype(F32) - 1.5
    centre_y = (cell % 4).astype(F32) - 1.5
    lane = lax.broadcasted_iota(jnp.int32, (16, slots), 1)
    low_ids = lax.broadcasted_iota(jnp.int32, (256, slots), 0)

    def one_tile(tile, carry):
        near = near_ref[0, pl.ds(tile, 1), :]
        along_x = place_ref[0, 0, pl.ds(tile, 1), :] - centre_x
        along_y = place_ref[0, 1, pl.ds(tile, 1), :] - centre_y
        along_z = place_ref[0, 2, pl.ds(tile, 1), :]
        values = jnp.exp(-0.5 * (along_x * along_x + along_y * along_y + along_z * along_z))
        values = jnp.where(lane < fill_ref[plane, tile], values, 0.0)
        start = pl.multiple_of(tile * 16, 16)
        denom_ref[pl.ds(start, 16), :] = jnp.broadcast_to(
            1.0 + jnp.sum(values, axis=1, keepdims=True), (16, 128)
        )
        half = values.astype(BF).astype(F32)
        high = jnp.broadcast_to(near >> 8, (16, slots))
        low = near & 255
        stacked = jnp.concatenate(
            [jnp.where(high == g, half, 0.0).astype(BF) for g in range(groups)], axis=0
        )
        hot = jnp.where(low_ids == low, 1.0, 0.0).astype(BF)
        block = lax.dot_general(
            stacked, hot, (((1,), (1,)), ((), ())), preferred_element_type=F32
        ).astype(BF)
        for g in range(groups):
            rows = block[g * 16 : g * 16 + 16, :]
            if g * 256 < split:
                close[pl.ds(start, 16), g * 256 : g * 256 + 256] = rows
            else:
                out_ref[pl.ds(start, 16), g * 256 - split : g * 256 - split + 256] = rows
        return carry

    lax.fori_loop(0, tiles, one_tile, 0, unroll=4)
    part_ref[...] = jnp.dot(
        close[:, :capacity], t0[...], preferred_element_type=F32
    ) + jnp.dot(close[:, capacity:], t1[...], preferred_element_type=F32)


def spread_weights(near, fill, place, owners, listed, feats, table):
    planes, tiles, slots = near.shape
    capacity, channels = table.shape
    rows = 2 * capacity
    return pl.pallas_call(
        spread_kernel,
        grid=(planes,),
        in_specs=[
            pl.BlockSpec(memory_space=pltpu.SMEM),
            pl.BlockSpec(memory_space=pltpu.SMEM),
            pl.BlockSpec((1, tiles, slots), lambda z: (z, 0, 0)),
            pl.BlockSpec((1, 3, tiles, slots), lambda z: (z, 0, 0, 0)),
        ]
        + [
            pl.BlockSpec(listed.shape, lambda z: (0, 0, 0)),
            pl.BlockSpec(feats.shape, lambda z: (0, 0)),
            pl.BlockSpec((capacity, channels), lambda z: (0, 0)),
        ],
        out_specs=[
            pl.BlockSpec((tiles * 16, rows), lambda z: (z, 0)),
            pl.BlockSpec((tiles * 16, channels), lambda z: (z, 0)),
            pl.BlockSpec((tiles * 16, 128), lambda z: (z, 0)),
        ],
        out_shape=[
            jax.ShapeDtypeStruct((planes * tiles * 16, rows), BF),
            jax.ShapeDtypeStruct((planes * tiles * 16, channels), F32),
            jax.ShapeDtypeStruct((planes * tiles * 16, 128), F32),
        ],
        scratch_shapes=[
            pltpu.VMEM((tiles * 16, rows), BF),
            pltpu.VMEM((capacity, channels), BF),
        ],
        compiler_params=pltpu.CompilerParams(vmem_limit_bytes=22 << 20),
    )(fill, owners, near, place, listed, feats, table)


def latent_kernel(
    flags_ref, spread_ref, part_ref, denom_ref, t0, t1,
    out_ref, near_ref, far_ref, first_ref, second_ref, total, order,
):
    plane = pl.program_id(0)
    last = pl.num_programs(0) - 1
    core = flags_ref[0]
    odd = flags_ref[2]
    capacity, channels = t0.shape
    cells = spread_ref.shape[0]
    tiles = cells // 16
    summed = part_ref[...]
    for place, table in ((0, t0), (1, t1)):
        summed = summed + jnp.dot(
            spread_ref[:, place * capacity : (place + 1) * capacity],
            table[...],
            preferred_element_type=F32,
        )
    for lanes in range(0, channels, 128):
        part = slice(lanes, lanes + 128)
        total[...] = summed[:, part] / denom_ref[...]
        for u in range(4):
            for v in range(4):
                order[pl.ds(v, tiles, stride=4), :] = total[
                    pl.ds(u * 4 + v, tiles, stride=16), :
                ]
            out_ref[0, u, :, part] = order[...].astype(BF)
    first_ref[0, 0] = out_ref[0, 3 * (1 - odd)]
    second_ref[0, 0] = out_ref[0, 3 * odd]

    @pl.when(plane == (1 - core) * last)
    def _():
        near_ref[...] = out_ref[...]

    @pl.when(plane == core * last)
    def _():
        far_ref[...] = out_ref[...]


def latent_block(flags, spread, part, denom, tables):
    cells = spread.shape[0]
    planes = 4
    per_plane = cells // planes
    capacity, channels = tables[0].shape
    width = per_plane // 4
    whole = pl.BlockSpec((capacity, channels), lambda z: (0, 0))
    plane_spec = pl.BlockSpec((1, 4, width, channels), lambda z: (0, 0, 0, 0))
    row_spec = pl.BlockSpec((1, 1, width, channels), lambda z: (z, 0, 0, 0))
    return pl.pallas_call(
        latent_kernel,
        grid=(planes,),
        in_specs=[
            pl.BlockSpec(memory_space=pltpu.SMEM),
            pl.BlockSpec((per_plane, spread.shape[1]), lambda z: (z, 0)),
            pl.BlockSpec((per_plane, channels), lambda z: (z, 0)),
            pl.BlockSpec((per_plane, 128), lambda z: (z, 0)),
        ]
        + [whole] * 2,
        out_specs=[
            pl.BlockSpec((1, 4, width, channels), lambda z: (z, 0, 0, 0)),
            plane_spec,
            plane_spec,
            row_spec,
            row_spec,
        ],
        out_shape=[
            jax.ShapeDtypeStruct((planes, 4, width, channels), BF),
            jax.ShapeDtypeStruct((1, 4, width, channels), BF),
            jax.ShapeDtypeStruct((1, 4, width, channels), BF),
            jax.ShapeDtypeStruct((planes, 1, width, channels), BF),
            jax.ShapeDtypeStruct((planes, 1, width, channels), BF),
        ],
        scratch_shapes=[
            pltpu.VMEM((per_plane, 128), F32),
            pltpu.VMEM((width, 128), F32),
        ],
        compiler_params=pltpu.CompilerParams(vmem_limit_bytes=20 << 20),
    )(flags, spread, part, denom, *tables)


def with_shifts(taps_ref, start, width, channels, y_ids):
    rows = pl.ds(start, width)
    low = pltpu.roll(taps_ref[rows, 0:channels], 1, 0)
    high = pltpu.roll(taps_ref[rows, 2 * channels :], width - 1, 0)
    return (
        jnp.where(y_ids == 0, 0.0, low)
        + taps_ref[rows, channels : 2 * channels]
        + jnp.where(y_ids == width - 1, 0.0, high)
    )


def times_weight(taps_ref, pieces, weight_ref, positions, channels):
    patch = jnp.concatenate(pieces, axis=1)
    for dy in range(3):
        matrix = jnp.concatenate([weight_ref[p + dy] for p in positions], axis=0)
        taps_ref[:, dy * channels : (dy + 1) * channels] = jnp.dot(
            patch, matrix, preferred_element_type=F32
        )


def inner_kernel(chosen, latent_ref, weight_ref, part_ref, padded, taps):
    planes, rows_x, width, channels = latent_ref.shape
    flat = rows_x * width
    none = jnp.zeros((planes, width, channels), BF)
    padded[:, 0] = none
    padded[:, 1 : rows_x + 1] = latent_ref[...]
    padded[:, rows_x + 1] = none
    y_ids = lax.broadcasted_iota(jnp.int32, (width, channels), 0)
    for place, z in enumerate(chosen):
        reach = [(dz, dx) for dz in range(3) if 0 <= z + dz - 1 < planes for dx in range(3)]
        pieces = [
            padded[z + dz - 1, dx : dx + rows_x].reshape(flat, channels) for dz, dx in reach
        ]
        times_weight(
            taps, pieces, weight_ref, [9 * dz + 3 * dx for dz, dx in reach], channels
        )
        for x in range(rows_x):
            part_ref[place, x] = with_shifts(taps, x * width, width, channels, y_ids)


def inner_conv(chosen, latent, weight):
    planes, rows_x, width, channels = latent.shape
    whole = pl.BlockSpec(memory_space=pltpu.VMEM)
    return pl.pallas_call(
        functools.partial(inner_kernel, chosen),
        in_specs=[whole] * 2,
        out_specs=whole,
        out_shape=jax.ShapeDtypeStruct((len(chosen), rows_x, width, channels), F32),
        scratch_shapes=[
            pltpu.VMEM((planes, rows_x + 2, width, channels), BF),
            pltpu.VMEM((rows_x * width, 3 * channels), F32),
        ],
        compiler_params=pltpu.CompilerParams(vmem_limit_bytes=20 << 20),
        cost_estimate=BRIEF,
    )(latent, weight)


def grad_taps(first, count, core, turned, shifted, keep_ref, give_ref, width):
    planes = turned.shape[0] - 2
    channels = turned.shape[1]
    flat = shifted.shape[0] // planes
    half_size = keep_ref.shape[1]

    def one_tap(index, carry):
        tap = first + index
        dz = tap // 3
        start = pl.multiple_of((tap % 3) * width, width)
        pieces = [turned[z + dz, :, pl.ds(start, flat)] for z in range(planes)]
        sums = jnp.dot(
            jnp.concatenate(pieces, axis=1), shifted[...], preferred_element_type=F32
        )
        for dy in range(3):
            part = sums[:, dy * channels : (dy + 1) * channels]
            both = jnp.concatenate(
                [
                    part[:, :128].reshape(channels // 8, 8, 128),
                    part[:, 128:].reshape(channels // 8, 8, 128),
                ],
                axis=1,
            )
            position = index * 3 + dy
            half = position // half_size
            slot = position - half * half_size
            rounded = both.astype(BF)

            @pl.when(half == core)
            def _():
                keep_ref[:, slot] = rounded

            @pl.when(half != core)
            def _():
                give_ref[:, slot] = rounded

        return carry

    lax.fori_loop(0, count, one_tap, 0)
    if 3 * count < 2 * half_size:
        unused = jnp.zeros((channels // 8, 16, 128), BF)

        @pl.when(core == 1)
        def _():
            keep_ref[:, half_size - 1] = unused

        @pl.when(core == 0)
        def _():
            give_ref[:, half_size - 1] = unused


def outer_kernel(
    flags_ref, middle_ref, edge_ref, latent_ref, near_ref, far_ref, first_ref, second_ref,
    first_end_ref, second_end_ref, weight_ref, bias_ref, cotangent_ref,
    act_ref, turned, shifted, keep_ref, give_ref,
    padded, rims, side_x, side_z,
):
    planes, rows_x, width, channels = latent_ref.shape
    flat = rows_x * width
    core = flags_ref[0]
    has_far = flags_ref[1] > 0
    odd = flags_ref[2]
    has_second = flags_ref[3] > 0
    near_z = (1 - core) * (planes + 1)
    far_z = core * (planes + 1)
    first_x = (1 - odd) * (rows_x + 1)
    second_x = odd * (rows_x + 1)
    none = jnp.zeros((), BF)
    padded[1 : planes + 1, 1 : rows_x + 1] = latent_ref[...]
    padded[near_z, 1 : rows_x + 1] = near_ref[0]
    padded[far_z, 1 : rows_x + 1] = jnp.where(has_far, far_ref[0], none)
    for x, face_ref, end_ref, present in (
        (first_x, first_ref, first_end_ref, True),
        (second_x, second_ref, second_end_ref, has_second),
    ):
        padded[1 : planes + 1, x] = jnp.where(present, face_ref[:, 0], none)
        padded[near_z, x] = jnp.where(present, end_ref[0], none)
        padded[far_z, x] = jnp.where(jnp.logical_and(present, has_far), end_ref[1], none)
    blank = jnp.zeros((width, channels), BF)
    for side in range(2):
        rims[side, 0] = blank
        rims[side, 1 : rows_x + 1] = padded[side * (planes + 1), 1 : rows_x + 1]
        rims[side, rows_x + 1] = blank
    y_ids = lax.broadcasted_iota(jnp.int32, (width, channels), 0)
    root = math.sqrt(2.0 / math.pi)

    def turn(z, carry):
        turned[z] = padded[z].reshape((rows_x + 2) * width, channels).T
        return carry

    lax.fori_loop(0, planes + 2, turn, 0)

    for side in range(2):
        column = side * (rows_x + 1)
        times_weight(
            side_x.at[side],
            [padded[dz : dz + planes, column].reshape(planes * width, channels) for dz in range(3)],
            weight_ref,
            [9 * dz + 6 * side for dz in range(3)],
            channels,
        )
        times_weight(
            side_z.at[side],
            [rims[side, dx : dx + rows_x].reshape(flat, channels) for dx in range(3)],
            weight_ref,
            [18 * side + 3 * dx for dx in range(3)],
            channels,
        )
    for z in range(planes):
        for x in range(rows_x):
            inner_part = middle_ref[0, x] if z == 1 else edge_ref[max(z - 1, 0), x]
            pre = inner_part + bias_ref[...]
            if x in (0, rows_x - 1):
                pre = pre + with_shifts(
                    side_x.at[int(x > 0)], z * width, width, channels, y_ids
                )
            if z in (0, planes - 1):
                pre = pre + with_shifts(
                    side_z.at[int(z > 0)], x * width, width, channels, y_ids
                )
            square = pre * pre
            inner = root * (pre + 0.044715 * (square * pre))
            bent = jnp.tanh(inner)
            gate = 0.5 * (1.0 + bent)
            act_ref[z, x] = (pre * gate).astype(BF)
            slope = gate + 0.5 * pre * (1.0 - bent * bent) * (
                root * (1.0 + 3.0 * 0.044715 * square)
            )
            grad = (cotangent_ref[z, x].astype(F32) * slope).astype(BF).astype(F32)
            rows = pl.ds(z * flat + x * width, width)
            shifted[rows, 0:channels] = jnp.where(
                y_ids == width - 1, 0.0, pltpu.roll(grad, width - 1, 0)
            ).astype(BF)
            shifted[rows, channels : 2 * channels] = grad.astype(BF)
            shifted[rows, 2 * channels :] = jnp.where(
                y_ids == 0, 0.0, pltpu.roll(grad, 1, 0)
            ).astype(BF)
    grad_taps(0, 5, core, turned, shifted, keep_ref, give_ref, width)


def outer_conv(flags, parts, latent, near, far, faces, weight, bias, cotangent):
    planes, rows_x, width, channels = latent.shape
    flat = rows_x * width
    whole = pl.BlockSpec(memory_space=pltpu.VMEM)
    half_terms = jax.ShapeDtypeStruct((channels // 8, 8, 16, 128), BF)
    return pl.pallas_call(
        outer_kernel,
        in_specs=[pl.BlockSpec(memory_space=pltpu.SMEM)] + [whole] * 12,
        out_specs=[whole] * 5,
        out_shape=[
            jax.ShapeDtypeStruct(latent.shape, BF),
            jax.ShapeDtypeStruct((planes + 2, channels, (rows_x + 2) * width), BF),
            jax.ShapeDtypeStruct((planes * flat, 3 * channels), BF),
            half_terms,
            half_terms,
        ],
        scratch_shapes=[
            pltpu.VMEM((planes + 2, rows_x + 2, width, channels), BF),
            pltpu.VMEM((2, rows_x + 2, width, channels), BF),
            pltpu.VMEM((2, planes * width, 3 * channels), F32),
            pltpu.VMEM((2, flat, 3 * channels), F32),
        ],
        compiler_params=pltpu.CompilerParams(vmem_limit_bytes=32 << 20),
    )(flags, *parts, latent, near, far, *faces, weight, bias, cotangent)


def rest_kernel(flags_ref, turned, shifted, keep_ref, give_ref):
    width = turned.shape[2] // 6
    grad_taps(5, 4, flags_ref[0], turned, shifted, keep_ref, give_ref, width)


def rest_terms(flags, turned, shifted):
    channels = turned.shape[1]
    whole = pl.BlockSpec(memory_space=pltpu.VMEM)
    half_terms = jax.ShapeDtypeStruct((channels // 8, 6, 16, 128), BF)
    return pl.pallas_call(
        rest_kernel,
        in_specs=[pl.BlockSpec(memory_space=pltpu.SMEM)] + [whole] * 2,
        out_specs=[whole] * 2,
        out_shape=[half_terms] * 2,
        compiler_params=pltpu.CompilerParams(vmem_limit_bytes=20 << 20),
    )(flags, turned, shifted)


def pair_sum(keep, give, swap):
    paired = keep.astype(F32) + lax.ppermute(give, "space", swap).astype(F32)
    return paired.astype(BF).reshape((2, 4, 4) + keep.shape[1:])


def sum_over(block, step, count, dim):
    chans = lax.axis_size("chan")
    index = lax.rem(lax.axis_index("chan") // step, count)
    total = lax.dynamic_index_in_dim(block, index, dim, keepdims=False).astype(F32)
    for offset in range(1, count):
        part = lax.dynamic_index_in_dim(block, index ^ offset, dim, keepdims=False)
        total = total + lax.ppermute(
            part, "chan", [(i, i ^ (offset * step)) for i in range(chans)]
        ).astype(F32)
    return total


def chan_pieces(array, step, count):
    chans = lax.axis_size("chan")
    return [array] + [
        lax.ppermute(array, "chan", [(i, i ^ (offset * step)) for i in range(chans)])
        for offset in range(1, count)
    ]


def in_place(index, pieces):
    result = jnp.zeros((len(pieces),) + pieces[0].shape, BF)
    for offset, piece in enumerate(pieces):
        result = lax.dynamic_update_index_in_dim(result, piece, index ^ offset, 0)
    return result


def in_order(core, own, other):
    low = jnp.where(core == 0, own, other)
    high = jnp.where(core == 0, other, own)
    return low, high


def on_device(
    point_feats,
    send_slots,
    send_counts,
    neighbors,
    tile_fill,
    offsets,
    weight,
    conv_bias,
    cotangent,
):
    spaces = lax.axis_size("space")
    chans = lax.axis_size("chan")
    planes, rows_x, width_y, channels = cotangent.shape
    row_count = weight.shape[0]
    space = lax.axis_index("space")
    chan = lax.axis_index("chan")
    core = lax.rem(space, 2)
    swap = [(i, i ^ 1) for i in range(spaces)]
    far = [(i, i ^ 2) for i in range(spaces)]
    cross = [(i, i ^ 3) for i in range(spaces)]
    first_pairs = [(i, i ^ 1) for i in range(chans)]
    second_pairs = [(i, (i - 1 + 2 * (i % 2)) % chans) for i in range(chans)]
    flags = jnp.stack(
        [
            core,
            jnp.logical_or(space == 1, space == 2).astype(jnp.int32),
            lax.rem(chan, 2),
            jnp.logical_and(chan > 0, chan < chans - 1).astype(jnp.int32),
        ]
    )

    taps = jnp.pad(weight.transpose(1, 0, 2), ((0, 1), (0, 0), (0, 0)))
    gathered = lax.dynamic_slice_in_dim(taps, core * 14, 14, 0)
    gathered = in_place(chan // 16, chan_pieces(gathered, 16, 2))

    slots, counts = send_slots[0, 0], send_counts[0, 0]
    capacity = slots.shape[1]
    listed = jnp.arange(capacity, dtype=jnp.int32) < counts[:, None]
    slots = jnp.where(listed, slots, -1).reshape(spaces, capacity // 128, 128)
    owners = space ^ jnp.arange(spaces, dtype=jnp.int32)
    to_other, to_far, to_cross = gather_listed(point_feats, slots, owners)
    to_far, to_cross, gathered = lax.optimization_barrier((to_far, to_cross, gathered))
    from_far = lax.ppermute(to_far, "space", far)
    from_cross = lax.ppermute(to_cross, "space", cross)
    from_other = lax.ppermute(to_other, "space", swap)
    gathered = jnp.broadcast_to(gathered[None], (16,) + gathered.shape)
    gathered = lax.all_to_all(
        gathered,
        "chan",
        split_axis=0,
        concat_axis=0,
        axis_index_groups=[[16 * y + i for i in range(16)] for y in range(chans // 16)],
        tiled=True,
    )
    near, _ = lax.optimization_barrier((neighbors[:, 0], to_far))
    spread, close_part, denom = spread_weights(
        near ^ (space * capacity),
        tile_fill[:, 0],
        offsets[:, 0].transpose(0, 2, 1, 3),
        owners,
        slots,
        point_feats,
        from_other,
    )

    latent, near_plane, far_plane, first_row, second_row = latent_block(
        flags, spread, close_part, denom, (from_far, from_cross)
    )

    far_rim = lax.ppermute(far_plane, "space", cross)
    near_rim = lax.ppermute(near_plane, "space", swap)
    gathered, _ = lax.optimization_barrier((gathered, near_plane))
    gathered = jnp.stack(in_order(core, gathered, lax.ppermute(gathered, "space", swap)))
    full_weight = gathered.transpose(0, 3, 2, 1, 4, 5).reshape(28, channels, channels)
    faces = [
        lax.ppermute(first_row, "chan", first_pairs),
        lax.ppermute(second_row, "chan", second_pairs),
    ]
    middle = inner_conv((1,), latent, full_weight)
    far_rim, near_rim, middle = lax.optimization_barrier((far_rim, near_rim, middle))
    odd = lax.rem(chan, 2)
    corners = []
    for side, pairs in ((1 - odd, first_pairs), (odd, second_pairs)):
        ends = [
            lax.dynamic_index_in_dim(rim, (rows_x - 1) * side, 1, keepdims=False)
            for rim in (near_rim, far_rim)
        ]
        ends = jnp.concatenate(ends, axis=0)
        corners.append(lax.ppermute(ends, "chan", pairs))
        held_latent = lax.optimization_barrier((latent, ends))[0]
    edge = inner_conv((0, 2, 3), held_latent, full_weight)

    activated, turned, shifted, keep, give = outer_conv(
        flags, (middle, edge), latent, near_rim, far_rim, (*faces, *corners),
        full_weight, conv_bias.astype(F32)[None], cotangent,
    )
    early = pair_sum(keep, give, swap)
    held_flags, early = lax.optimization_barrier((flags, early))
    late = pair_sum(*rest_terms(held_flags, turned, shifted), swap)
    early = sum_over(early, 1, 4, 2).astype(BF)
    late = sum_over(late, 4, 4, 1).astype(BF)
    early = sum_over(early, 4, 4, 1)
    late = sum_over(late, 1, 4, 1)
    both = jnp.concatenate([early, late], axis=1)
    y_low = chan // 16
    kept = lax.dynamic_index_in_dim(both, y_low, 0, keepdims=False)
    passed = lax.dynamic_index_in_dim(both, 1 - y_low, 0, keepdims=False).astype(BF)
    over = [(i, i ^ 16) for i in range(chans)]
    far_over = [(i, i ^ (2 * chans) ^ 16) for i in range(spaces * chans)]
    own_sum = (
        kept
        + lax.ppermute(passed, "chan", over).astype(F32)
        + lax.ppermute(passed, ("space", "chan"), far_over).astype(F32)
        + lax.ppermute(kept.astype(BF), "space", far).astype(F32)
    )
    low_sum, high_sum = in_order(core, own_sum, lax.ppermute(own_sum, "space", swap))
    total = jnp.concatenate([low_sum[:8], high_sum[:7], low_sum[8:], high_sum[8:]], axis=0)
    total = total.reshape(27, 2, row_count, channels // 2).transpose(2, 0, 1, 3)
    scaling = 1.0 / math.sqrt(planes * spaces * rows_x * chans * width_y)
    return (activated, total.reshape(row_count, 27, channels) * scaling)


def solution(mesh):
    return jax.shard_map(
        on_device,
        mesh=mesh,
        in_specs=(
            P(("space", "chan"), None),
            P("space", "chan", None, None),
            P("space", "chan", None),
            P("space", "chan", None, None),
            P("space", "chan", None),
            P("space", "chan", None, None, None),
            P("chan", None, None),
            P(),
            P("space", "chan", None, None),
        ),
        out_specs=(P("space", "chan", None, None), P("chan", None, None)),
        check_vma=False,
    )
```

```python
import functools
import math

import jax
import jax.numpy as jnp
from jax import lax
from jax.experimental import pallas as pl
from jax.experimental.pallas import tpu as pltpu
from jax.sharding import PartitionSpec as P

BF = jnp.bfloat16
F32 = jnp.float32
BRIEF = pl.CostEstimate(flops=1, bytes_accessed=1, transcendentals=0)


def listed_rows(slots, feats_ref, out_ref):
    points = feats_ref.shape[0]
    point_ids = lax.broadcasted_iota(jnp.int32, (128, points), 1)
    columns = slots.T
    for half in range(2):
        hot = [
            jnp.where(point_ids == columns[:, r : r + 1], 1.0, 0.0).astype(BF)
            for r in range(half * 4, half * 4 + 4)
        ]
        rows = jnp.dot(
            jnp.concatenate(hot, axis=0), feats_ref[...], preferred_element_type=F32
        )
        out_ref[half * 512 : half * 512 + 512, :] = rows.astype(BF)


def send_kernel(owners_ref, slots_ref, feats_ref, *out_refs):
    for place, out_ref in enumerate(out_refs):
        listed_rows(slots_ref[owners_ref[place + 1]], feats_ref, out_ref)


def gather_listed(feats, slots, owners):
    count, rows, lanes = slots.shape
    whole = pl.BlockSpec(memory_space=pltpu.VMEM)
    return pl.pallas_call(
        send_kernel,
        in_specs=[pl.BlockSpec(memory_space=pltpu.SMEM), whole, whole],
        out_specs=[whole] * (count - 1),
        out_shape=[jax.ShapeDtypeStruct((rows * lanes, feats.shape[1]), BF)] * (count - 1),
        compiler_params=pltpu.CompilerParams(vmem_limit_bytes=16 << 20),
        cost_estimate=BRIEF,
    )(owners, slots, feats)


def spread_kernel(
    fill_ref, owners_ref, near_ref, place_ref, slots_ref, feats_ref, t1,
    out_ref, part_ref, denom_ref, close, t0,
):
    plane = pl.program_id(0)
    tiles = near_ref.shape[1]
    slots = near_ref.shape[2]
    groups = (out_ref.shape[1] + close.shape[1]) // 256
    split = close.shape[1]
    capacity = t0.shape[0]

    @pl.when(plane == 0)
    def _():
        listed_rows(slots_ref[owners_ref[0]], feats_ref, t0)

    cell = lax.broadcasted_iota(jnp.int32, (16, slots), 0)
    centre_x = (cell // 4).astype(F32) - 1.5
    centre_y = (cell % 4).astype(F32) - 1.5
    lane = lax.broadcasted_iota(jnp.int32, (16, slots), 1)
    low_ids = lax.broadcasted_iota(jnp.int32, (256, slots), 0)

    def one_tile(tile, carry):
        near = near_ref[0, pl.ds(tile, 1), :]
        along_x = place_ref[0, 0, pl.ds(tile, 1), :] - centre_x
        along_y = place_ref[0, 1, pl.ds(tile, 1), :] - centre_y
        along_z = place_ref[0, 2, pl.ds(tile, 1), :]
        values = jnp.exp(-0.5 * (along_x * along_x + along_y * along_y + along_z * along_z))
        values = jnp.where(lane < fill_ref[plane, tile], values, 0.0)
        start = pl.multiple_of(tile * 16, 16)
        denom_ref[pl.ds(start, 16), :] = jnp.broadcast_to(
            1.0 + jnp.sum(values, axis=1, keepdims=True), (16, 128)
        )
        half = values.astype(BF).astype(F32)
        high = jnp.broadcast_to(near >> 8, (16, slots))
        low = near & 255
        stacked = jnp.concatenate(
            [jnp.where(high == g, half, 0.0).astype(BF) for g in range(groups)], axis=0
        )
        hot = jnp.where(low_ids == low, 1.0, 0.0).astype(BF)
        block = lax.dot_general(
            stacked, hot, (((1,), (1,)), ((), ())), preferred_element_type=F32
        ).astype(BF)
        for g in range(groups):
            rows = block[g * 16 : g * 16 + 16, :]
            if g * 256 < split:
                close[pl.ds(start, 16), g * 256 : g * 256 + 256] = rows
            else:
                out_ref[pl.ds(start, 16), g * 256 - split : g * 256 - split + 256] = rows
        return carry

    lax.fori_loop(0, tiles, one_tile, 0, unroll=4)
    part_ref[...] = jnp.dot(
        close[:, :capacity], t0[...], preferred_element_type=F32
    ) + jnp.dot(close[:, capacity:], t1[...], preferred_element_type=F32)


def spread_weights(near, fill, place, owners, listed, feats, table):
    planes, tiles, slots = near.shape
    capacity, channels = table.shape
    rows = 2 * capacity
    return pl.pallas_call(
        spread_kernel,
        grid=(planes,),
        in_specs=[
            pl.BlockSpec(memory_space=pltpu.SMEM),
            pl.BlockSpec(memory_space=pltpu.SMEM),
            pl.BlockSpec((1, tiles, slots), lambda z: (z, 0, 0)),
            pl.BlockSpec((1, 3, tiles, slots), lambda z: (z, 0, 0, 0)),
        ]
        + [
            pl.BlockSpec(listed.shape, lambda z: (0, 0, 0)),
            pl.BlockSpec(feats.shape, lambda z: (0, 0)),
            pl.BlockSpec((capacity, channels), lambda z: (0, 0)),
        ],
        out_specs=[
            pl.BlockSpec((tiles * 16, rows), lambda z: (z, 0)),
            pl.BlockSpec((tiles * 16, channels), lambda z: (z, 0)),
            pl.BlockSpec((tiles * 16, 128), lambda z: (z, 0)),
        ],
        out_shape=[
            jax.ShapeDtypeStruct((planes * tiles * 16, rows), BF),
            jax.ShapeDtypeStruct((planes * tiles * 16, channels), F32),
            jax.ShapeDtypeStruct((planes * tiles * 16, 128), F32),
        ],
        scratch_shapes=[
            pltpu.VMEM((tiles * 16, rows), BF),
            pltpu.VMEM((capacity, channels), BF),
        ],
        compiler_params=pltpu.CompilerParams(vmem_limit_bytes=22 << 20),
    )(fill, owners, near, place, listed, feats, table)


def latent_kernel(
    flags_ref, spread_ref, part_ref, denom_ref, t0, t1,
    out_ref, near_ref, far_ref, first_ref, second_ref, total, order,
):
    plane = pl.program_id(0)
    last = pl.num_programs(0) - 1
    core = flags_ref[0]
    odd = flags_ref[2]
    capacity, channels = t0.shape
    cells = spread_ref.shape[0]
    tiles = cells // 16
    summed = part_ref[...]
    for place, table in ((0, t0), (1, t1)):
        summed = summed + jnp.dot(
            spread_ref[:, place * capacity : (place + 1) * capacity],
            table[...],
            preferred_element_type=F32,
        )
    for lanes in range(0, channels, 128):
        part = slice(lanes, lanes + 128)
        total[...] = summed[:, part] / denom_ref[...]
        for u in range(4):
            for v in range(4):
                order[pl.ds(v, tiles, stride=4), :] = total[
                    pl.ds(u * 4 + v, tiles, stride=16), :
                ]
            out_ref[0, u, :, part] = order[...].astype(BF)
    first_ref[0, 0] = out_ref[0, 3 * (1 - odd)]
    second_ref[0, 0] = out_ref[0, 3 * odd]

    @pl.when(plane == (1 - core) * last)
    def _():
        near_ref[...] = out_ref[...]

    @pl.when(plane == core * last)
    def _():
        far_ref[...] = out_ref[...]


def latent_block(flags, spread, part, denom, tables):
    cells = spread.shape[0]
    planes = 4
    per_plane = cells // planes
    capacity, channels = tables[0].shape
    width = per_plane // 4
    whole = pl.BlockSpec((capacity, channels), lambda z: (0, 0))
    plane_spec = pl.BlockSpec((1, 4, width, channels), lambda z: (0, 0, 0, 0))
    row_spec = pl.BlockSpec((1, 1, width, channels), lambda z: (z, 0, 0, 0))
    return pl.pallas_call(
        latent_kernel,
        grid=(planes,),
        in_specs=[
            pl.BlockSpec(memory_space=pltpu.SMEM),
            pl.BlockSpec((per_plane, spread.shape[1]), lambda z: (z, 0)),
            pl.BlockSpec((per_plane, channels), lambda z: (z, 0)),
            pl.BlockSpec((per_plane, 128), lambda z: (z, 0)),
        ]
        + [whole] * 2,
        out_specs=[
            pl.BlockSpec((1, 4, width, channels), lambda z: (z, 0, 0, 0)),
            plane_spec,
            plane_spec,
            row_spec,
            row_spec,
        ],
        out_shape=[
            jax.ShapeDtypeStruct((planes, 4, width, channels), BF),
            jax.ShapeDtypeStruct((1, 4, width, channels), BF),
            jax.ShapeDtypeStruct((1, 4, width, channels), BF),
            jax.ShapeDtypeStruct((planes, 1, width, channels), BF),
            jax.ShapeDtypeStruct((planes, 1, width, channels), BF),
        ],
        scratch_shapes=[
            pltpu.VMEM((per_plane, 128), F32),
            pltpu.VMEM((width, 128), F32),
        ],
        compiler_params=pltpu.CompilerParams(vmem_limit_bytes=20 << 20),
    )(flags, spread, part, denom, *tables)


def with_shifts(taps_ref, start, width, channels, y_ids):
    rows = pl.ds(start, width)
    low = pltpu.roll(taps_ref[rows, 0:channels], 1, 0)
    high = pltpu.roll(taps_ref[rows, 2 * channels :], width - 1, 0)
    return (
        jnp.where(y_ids == 0, 0.0, low)
        + taps_ref[rows, channels : 2 * channels]
        + jnp.where(y_ids == width - 1, 0.0, high)
    )


def times_weight(taps_ref, pieces, weight_ref, positions, channels):
    patch = jnp.concatenate(pieces, axis=1)
    for dy in range(3):
        matrix = jnp.concatenate([weight_ref[p + dy] for p in positions], axis=0)
        taps_ref[:, dy * channels : (dy + 1) * channels] = jnp.dot(
            patch, matrix, preferred_element_type=F32
        )


def inner_kernel(chosen, latent_ref, weight_ref, part_ref, padded, taps):
    planes, rows_x, width, channels = latent_ref.shape
    flat = rows_x * width
    none = jnp.zeros((planes, width, channels), BF)
    padded[:, 0] = none
    padded[:, 1 : rows_x + 1] = latent_ref[...]
    padded[:, rows_x + 1] = none
    y_ids = lax.broadcasted_iota(jnp.int32, (width, channels), 0)
    for place, z in enumerate(chosen):
        reach = [(dz, dx) for dz in range(3) if 0 <= z + dz - 1 < planes for dx in range(3)]
        pieces = [
            padded[z + dz - 1, dx : dx + rows_x].reshape(flat, channels) for dz, dx in reach
        ]
        times_weight(
            taps, pieces, weight_ref, [9 * dz + 3 * dx for dz, dx in reach], channels
        )
        for x in range(rows_x):
            part_ref[place, x] = with_shifts(taps, x * width, width, channels, y_ids)


def inner_conv(chosen, latent, weight):
    planes, rows_x, width, channels = latent.shape
    whole = pl.BlockSpec(memory_space=pltpu.VMEM)
    return pl.pallas_call(
        functools.partial(inner_kernel, chosen),
        in_specs=[whole] * 2,
        out_specs=whole,
        out_shape=jax.ShapeDtypeStruct((len(chosen), rows_x, width, channels), F32),
        scratch_shapes=[
            pltpu.VMEM((planes, rows_x + 2, width, channels), BF),
            pltpu.VMEM((rows_x * width, 3 * channels), F32),
        ],
        compiler_params=pltpu.CompilerParams(vmem_limit_bytes=20 << 20),
        cost_estimate=BRIEF,
    )(latent, weight)


def grad_taps(first, count, core, turned, shifted, keep_ref, give_ref, width):
    planes = turned.shape[0] - 2
    channels = turned.shape[1]
    flat = shifted.shape[0] // planes
    half_size = keep_ref.shape[1]

    def one_tap(index, carry):
        tap = first + index
        dz = tap // 3
        start = pl.multiple_of((tap % 3) * width, width)
        pieces = [turned[z + dz, :, pl.ds(start, flat)] for z in range(planes)]
        sums = jnp.dot(
            jnp.concatenate(pieces, axis=1), shifted[...], preferred_element_type=F32
        )
        for dy in range(3):
            part = sums[:, dy * channels : (dy + 1) * channels]
            both = jnp.concatenate(
                [
                    part[:, :128].reshape(channels // 8, 8, 128),
                    part[:, 128:].reshape(channels // 8, 8, 128),
                ],
                axis=1,
            )
            position = index * 3 + dy
            half = position // half_size
            slot = position - half * half_size
            rounded = both.astype(BF)

            @pl.when(half == core)
            def _():
                keep_ref[:, slot] = rounded

            @pl.when(half != core)
            def _():
                give_ref[:, slot] = rounded

        return carry

    lax.fori_loop(0, count, one_tap, 0, unroll=True)
    if 3 * count < 2 * half_size:
        unused = jnp.zeros((channels // 8, 16, 128), BF)

        @pl.when(core == 1)
        def _():
            keep_ref[:, half_size - 1] = unused

        @pl.when(core == 0)
        def _():
            give_ref[:, half_size - 1] = unused


def outer_kernel(
    flags_ref, middle_ref, edge_ref, latent_ref, near_ref, far_ref, first_ref, second_ref,
    first_end_ref, second_end_ref, weight_ref, bias_ref, cotangent_ref,
    act_ref, turned, shifted, keep_ref, give_ref,
    padded, rims, side_x, side_z,
):
    planes, rows_x, width, channels = latent_ref.shape
    flat = rows_x * width
    core = flags_ref[0]
    has_far = flags_ref[1] > 0
    odd = flags_ref[2]
    has_second = flags_ref[3] > 0
    near_z = (1 - core) * (planes + 1)
    far_z = core * (planes + 1)
    first_x = (1 - odd) * (rows_x + 1)
    second_x = odd * (rows_x + 1)
    none = jnp.zeros((), BF)
    padded[1 : planes + 1, 1 : rows_x + 1] = latent_ref[...]
    padded[near_z, 1 : rows_x + 1] = near_ref[0]
    padded[far_z, 1 : rows_x + 1] = jnp.where(has_far, far_ref[0], none)
    for x, face_ref, end_ref, present in (
        (first_x, first_ref, first_end_ref, True),
        (second_x, second_ref, second_end_ref, has_second),
    ):
        padded[1 : planes + 1, x] = jnp.where(present, face_ref[:, 0], none)
        padded[near_z, x] = jnp.where(present, end_ref[0], none)
        padded[far_z, x] = jnp.where(jnp.logical_and(present, has_far), end_ref[1], none)
    blank = jnp.zeros((width, channels), BF)
    for side in range(2):
        rims[side, 0] = blank
        rims[side, 1 : rows_x + 1] = padded[side * (planes + 1), 1 : rows_x + 1]
        rims[side, rows_x + 1] = blank
    y_ids = lax.broadcasted_iota(jnp.int32, (width, channels), 0)
    root = math.sqrt(2.0 / math.pi)

    def turn(z, carry):
        turned[z] = padded[z].reshape((rows_x + 2) * width, channels).T
        return carry

    lax.fori_loop(0, planes + 2, turn, 0)

    for side in range(2):
        column = side * (rows_x + 1)
        times_weight(
            side_x.at[side],
            [padded[dz : dz + planes, column].reshape(planes * width, channels) for dz in range(3)],
            weight_ref,
            [9 * dz + 6 * side for dz in range(3)],
            channels,
        )
        times_weight(
            side_z.at[side],
            [rims[side, dx : dx + rows_x].reshape(flat, channels) for dx in range(3)],
            weight_ref,
            [18 * side + 3 * dx for dx in range(3)],
            channels,
        )
    for z in range(planes):
        for x in range(rows_x):
            inner_part = middle_ref[0, x] if z == 1 else edge_ref[max(z - 1, 0), x]
            pre = inner_part + bias_ref[...]
            if x in (0, rows_x - 1):
                pre = pre + with_shifts(
                    side_x.at[int(x > 0)], z * width, width, channels, y_ids
                )
            if z in (0, planes - 1):
                pre = pre + with_shifts(
                    side_z.at[int(z > 0)], x * width, width, channels, y_ids
                )
            square = pre * pre
            inner = root * (pre + 0.044715 * (square * pre))
            bent = jnp.tanh(inner)
            gate = 0.5 * (1.0 + bent)
            act_ref[z, x] = (pre * gate).astype(BF)
            slope = gate + 0.5 * pre * (1.0 - bent * bent) * (
                root * (1.0 + 3.0 * 0.044715 * square)
            )
            grad = (cotangent_ref[z, x].astype(F32) * slope).astype(BF).astype(F32)
            rows = pl.ds(z * flat + x * width, width)
            shifted[rows, 0:channels] = jnp.where(
                y_ids == width - 1, 0.0, pltpu.roll(grad, width - 1, 0)
            ).astype(BF)
            shifted[rows, channels : 2 * channels] = grad.astype(BF)
            shifted[rows, 2 * channels :] = jnp.where(
                y_ids == 0, 0.0, pltpu.roll(grad, 1, 0)
            ).astype(BF)
    grad_taps(0, 5, core, turned, shifted, keep_ref, give_ref, width)


def outer_conv(flags, parts, latent, near, far, faces, weight, bias, cotangent):
    planes, rows_x, width, channels = latent.shape
    flat = rows_x * width
    whole = pl.BlockSpec(memory_space=pltpu.VMEM)
    half_terms = jax.ShapeDtypeStruct((channels // 8, 8, 16, 128), BF)
    return pl.pallas_call(
        outer_kernel,
        in_specs=[pl.BlockSpec(memory_space=pltpu.SMEM)] + [whole] * 12,
        out_specs=[whole] * 5,
        out_shape=[
            jax.ShapeDtypeStruct(latent.shape, BF),
            jax.ShapeDtypeStruct((planes + 2, channels, (rows_x + 2) * width), BF),
            jax.ShapeDtypeStruct((planes * flat, 3 * channels), BF),
            half_terms,
            half_terms,
        ],
        scratch_shapes=[
            pltpu.VMEM((planes + 2, rows_x + 2, width, channels), BF),
            pltpu.VMEM((2, rows_x + 2, width, channels), BF),
            pltpu.VMEM((2, planes * width, 3 * channels), F32),
            pltpu.VMEM((2, flat, 3 * channels), F32),
        ],
        compiler_params=pltpu.CompilerParams(vmem_limit_bytes=32 << 20),
    )(flags, *parts, latent, near, far, *faces, weight, bias, cotangent)


def rest_kernel(flags_ref, turned, shifted, keep_ref, give_ref):
    width = turned.shape[2] // 6
    grad_taps(5, 4, flags_ref[0], turned, shifted, keep_ref, give_ref, width)


def rest_terms(flags, turned, shifted):
    channels = turned.shape[1]
    whole = pl.BlockSpec(memory_space=pltpu.VMEM)
    half_terms = jax.ShapeDtypeStruct((channels // 8, 6, 16, 128), BF)
    return pl.pallas_call(
        rest_kernel,
        in_specs=[pl.BlockSpec(memory_space=pltpu.SMEM)] + [whole] * 2,
        out_specs=[whole] * 2,
        out_shape=[half_terms] * 2,
        compiler_params=pltpu.CompilerParams(vmem_limit_bytes=20 << 20),
    )(flags, turned, shifted)


def pair_sum(keep, give, swap):
    paired = keep.astype(F32) + lax.ppermute(give, "space", swap).astype(F32)
    return paired.astype(BF).reshape((2, 4, 4) + keep.shape[1:])


def sum_over(block, step, count, dim):
    chans = lax.axis_size("chan")
    index = lax.rem(lax.axis_index("chan") // step, count)
    total = lax.dynamic_index_in_dim(block, index, dim, keepdims=False).astype(F32)
    for offset in range(1, count):
        part = lax.dynamic_index_in_dim(block, index ^ offset, dim, keepdims=False)
        total = total + lax.ppermute(
            part, "chan", [(i, i ^ (offset * step)) for i in range(chans)]
        ).astype(F32)
    return total


def chan_pieces(array, step, count):
    chans = lax.axis_size("chan")
    return [array] + [
        lax.ppermute(array, "chan", [(i, i ^ (offset * step)) for i in range(chans)])
        for offset in range(1, count)
    ]


def in_place(index, pieces):
    result = jnp.zeros((len(pieces),) + pieces[0].shape, BF)
    for offset, piece in enumerate(pieces):
        result = lax.dynamic_update_index_in_dim(result, piece, index ^ offset, 0)
    return result


def in_order(core, own, other):
    low = jnp.where(core == 0, own, other)
    high = jnp.where(core == 0, other, own)
    return low, high


def on_device(
    point_feats,
    send_slots,
    send_counts,
    neighbors,
    tile_fill,
    offsets,
    weight,
    conv_bias,
    cotangent,
):
    spaces = lax.axis_size("space")
    chans = lax.axis_size("chan")
    planes, rows_x, width_y, channels = cotangent.shape
    row_count = weight.shape[0]
    space = lax.axis_index("space")
    chan = lax.axis_index("chan")
    core = lax.rem(space, 2)
    swap = [(i, i ^ 1) for i in range(spaces)]
    far = [(i, i ^ 2) for i in range(spaces)]
    cross = [(i, i ^ 3) for i in range(spaces)]
    first_pairs = [(i, i ^ 1) for i in range(chans)]
    second_pairs = [(i, (i - 1 + 2 * (i % 2)) % chans) for i in range(chans)]
    flags = jnp.stack(
        [
            core,
            jnp.logical_or(space == 1, space == 2).astype(jnp.int32),
            lax.rem(chan, 2),
            jnp.logical_and(chan > 0, chan < chans - 1).astype(jnp.int32),
        ]
    )

    taps = jnp.pad(weight.transpose(1, 0, 2), ((0, 1), (0, 0), (0, 0)))
    gathered = lax.dynamic_slice_in_dim(taps, core * 14, 14, 0)
    gathered = in_place(chan // 16, chan_pieces(gathered, 16, 2))

    slots, counts = send_slots[0, 0], send_counts[0, 0]
    capacity = slots.shape[1]
    listed = jnp.arange(capacity, dtype=jnp.int32) < counts[:, None]
    slots = jnp.where(listed, slots, -1).reshape(spaces, capacity // 128, 128)
    owners = space ^ jnp.arange(spaces, dtype=jnp.int32)
    to_other, to_far, to_cross = gather_listed(point_feats, slots, owners)
    to_far, to_cross, gathered = lax.optimization_barrier((to_far, to_cross, gathered))
    from_far = lax.ppermute(to_far, "space", far)
    from_cross = lax.ppermute(to_cross, "space", cross)
    from_other = lax.ppermute(to_other, "space", swap)
    gathered = jnp.broadcast_to(gathered[None], (16,) + gathered.shape)
    gathered = lax.all_to_all(
        gathered,
        "chan",
        split_axis=0,
        concat_axis=0,
        axis_index_groups=[[16 * y + i for i in range(16)] for y in range(chans // 16)],
        tiled=True,
    )
    near, _ = lax.optimization_barrier((neighbors[:, 0], to_far))
    spread, close_part, denom = spread_weights(
        near ^ (space * capacity),
        tile_fill[:, 0],
        offsets[:, 0].transpose(0, 2, 1, 3),
        owners,
        slots,
        point_feats,
        from_other,
    )

    latent, near_plane, far_plane, first_row, second_row = latent_block(
        flags, spread, close_part, denom, (from_far, from_cross)
    )

    far_rim = lax.ppermute(far_plane, "space", cross)
    near_rim = lax.ppermute(near_plane, "space", swap)
    gathered, _ = lax.optimization_barrier((gathered, near_plane))
    gathered = jnp.stack(in_order(core, gathered, lax.ppermute(gathered, "space", swap)))
    full_weight = gathered.transpose(0, 3, 2, 1, 4, 5).reshape(28, channels, channels)
    faces = [
        lax.ppermute(first_row, "chan", first_pairs),
        lax.ppermute(second_row, "chan", second_pairs),
    ]
    middle = inner_conv((1,), latent, full_weight)
    far_rim, near_rim, middle = lax.optimization_barrier((far_rim, near_rim, middle))
    odd = lax.rem(chan, 2)
    corners = []
    for side, pairs in ((1 - odd, first_pairs), (odd, second_pairs)):
        ends = [
            lax.dynamic_index_in_dim(rim, (rows_x - 1) * side, 1, keepdims=False)
            for rim in (near_rim, far_rim)
        ]
        ends = jnp.concatenate(ends, axis=0)
        corners.append(lax.ppermute(ends, "chan", pairs))
        held_latent = lax.optimization_barrier((latent, ends))[0]
    edge = inner_conv((0, 2, 3), held_latent, full_weight)

    activated, turned, shifted, keep, give = outer_conv(
        flags, (middle, edge), latent, near_rim, far_rim, (*faces, *corners),
        full_weight, conv_bias.astype(F32)[None], cotangent,
    )
    early = pair_sum(keep, give, swap)
    held_flags, early = lax.optimization_barrier((flags, early))
    late = pair_sum(*rest_terms(held_flags, turned, shifted), swap)
    early = sum_over(early, 1, 4, 2).astype(BF)
    late = sum_over(late, 4, 4, 1).astype(BF)
    early = sum_over(early, 4, 4, 1)
    late = sum_over(late, 1, 4, 1)
    both = jnp.concatenate([early, late], axis=1)
    y_low = chan // 16
    kept = lax.dynamic_index_in_dim(both, y_low, 0, keepdims=False)
    passed = lax.dynamic_index_in_dim(both, 1 - y_low, 0, keepdims=False).astype(BF)
    over = [(i, i ^ 16) for i in range(chans)]
    far_over = [(i, i ^ (2 * chans) ^ 16) for i in range(spaces * chans)]
    own_sum = (
        kept
        + lax.ppermute(passed, "chan", over).astype(F32)
        + lax.ppermute(passed, ("space", "chan"), far_over).astype(F32)
        + lax.ppermute(kept.astype(BF), "space", far).astype(F32)
    )
    low_sum, high_sum = in_order(core, own_sum, lax.ppermute(own_sum, "space", swap))
    total = jnp.concatenate([low_sum[:8], high_sum[:7], low_sum[8:], high_sum[8:]], axis=0)
    total = total.reshape(27, 2, row_count, channels // 2).transpose(2, 0, 1, 3)
    scaling = 1.0 / math.sqrt(planes * spaces * rows_x * chans * width_y)
    return (activated, total.reshape(row_count, 27, channels) * scaling)


def solution(mesh):
    return jax.shard_map(
        on_device,
        mesh=mesh,
        in_specs=(
            P(("space", "chan"), None),
            P("space", "chan", None, None),
            P("space", "chan", None),
            P("space", "chan", None, None),
            P("space", "chan", None),
            P("space", "chan", None, None, None),
            P("chan", None, None),
            P(),
            P("space", "chan", None, None),
        ),
        out_specs=(P("space", "chan", None, None), P("chan", None, None)),
        check_vma=False,
    )
```
